32 devices in a mesh: ctx: 8 (over y, x, core), head: 4 (over z).
Axes of the slice: x: 2, y: 2, z: 4, core: 2. Of those that a mesh axis runs over, the one named last changes fastest.
Arguments:
- query: bfloat16 [4096, 2048], P('ctx', 'head'), may hold values from -6 to 6
- key: bfloat16 [4096, 2048], P('ctx', 'head'), may hold values from -6 to 6
- value: bfloat16 [4096, 2048], P('ctx', 'head'), may hold values from -6 to 6
- out_grad: bfloat16 [4096, 2048], P('ctx', 'head'), may hold values from -6 to 6
- links: int32 [32, 6], replicated, may hold values from -1 to 29, as said below
Outputs:
- query_grad: bfloat16 [4096, 2048], P('ctx', 'head')
- key_grad: bfloat16 [4096, 2048], P('ctx', 'head')
- value_grad: bfloat16 [4096, 2048], P('ctx', 'head')
The draws below stay inside these ranges and needn't reach their ends.
Inputs may be any that keep to these rules, and one draw needn't show every extreme that they name: `links`: entry (b, s) is -1 or the index of a block at most b - 2. Over the 6 entries of all query blocks held by one index of ctx, at most 3 name blocks held by any one index of ctx (itself included), and on every index of ctx some index is named exactly 3 times.
All inputs are finite; a program needn't handle non-finite values.
Results may differ from the reference program's by a relative error of at most 0.01.
Values may be sent and summed in bfloat16 or wider, within the bound.
No kernel may reach another device: no remote copies, remote signals or barrier semaphores. Data moves between devices by JAX's collectives and lax.ppermute only.
A program may use at most 192 MiB of HBM per device.

```python
import jax
import jax.numpy as jnp
from jax import lax

HEADS = 16
HEAD_DIM = 128
BLK = 128
WIN = 2
LINKS = 6
TOK_DEV = 512
SHARDS = 8
SEQ = 4096
NBLK = 32
STRETCH_BLOCKS = 2
WIDTH = 2048
LINK_CAP = 3
N_CTX = 8


def storage_order(natural):
    half_rows = TOK_DEV // 2
    width = natural.shape[-1]
    first = natural[:SHARDS * half_rows].reshape(SHARDS, half_rows, width)
    second = natural[SHARDS * half_rows:].reshape(SHARDS, half_rows, width)[::-1]
    return jnp.stack((first, second), 1).reshape(-1, width)


def drawn_pair(key, part):
    base_query = jnp.clip(jax.random.normal(jax.random.fold_in(key, 11), (SEQ, WIDTH), jnp.float32), -6.0, 6.0)
    base_key = jnp.clip(jax.random.normal(jax.random.fold_in(key, 12), (SEQ, WIDTH), jnp.float32), -6.0, 6.0)
    return (storage_order(base_query).astype(jnp.bfloat16), storage_order(base_key).astype(jnp.bfloat16))


def draw_query(key, part):
    return drawn_pair(key, part)[0]


def draw_key(key, part):
    return drawn_pair(key, part)[1]


def draw_links(key, part):
    shards = SHARDS
    stretch_blocks = STRETCH_BLOCKS
    capacity = LINK_CAP
    entries = 2 * stretch_blocks * LINKS
    devices = jnp.arange(shards, dtype=jnp.int32)
    local_ids = jnp.arange(2 * stretch_blocks, dtype=jnp.int32)
    query_stretch = jnp.where(local_ids[None, :] < stretch_blocks, devices[:, None], 2 * shards - 1 - devices[:, None])
    query_block = query_stretch * stretch_blocks + local_ids[None, :] % stretch_blocks
    entry_block = jnp.repeat(query_block, LINKS, axis=1)
    entry_local = jnp.repeat(local_ids, LINKS)
    ordinal = jnp.arange(entries, dtype=jnp.int32)
    order_score = jax.random.randint(jax.random.fold_in(key, 21), (shards, entries), 0, 1 << 16) * entries + ordinal[None, :]
    order_score = order_score + jnp.where(entry_local[None, :] < stretch_blocks, entries << 16, 0)
    ordering = jnp.argsort(order_score, axis=1)
    position = jnp.argsort(ordering, axis=1).astype(jnp.int32)
    owner_score = jax.random.randint(jax.random.fold_in(key, 22), (shards, shards), 0, 1 << 16) * shards + devices[None, :]
    owner_perm = jnp.argsort(owner_score, axis=1).astype(jnp.int32)
    owner_dev = jnp.take_along_axis(owner_perm, position // capacity, axis=1)
    cand_stretch = jnp.where(local_ids[None, None, :] < stretch_blocks, owner_dev[:, :, None], 2 * shards - 1 - owner_dev[:, :, None])
    candidate = cand_stretch * stretch_blocks + local_ids[None, None, :] % stretch_blocks
    allowed = candidate <= entry_block[:, :, None] - WIN
    pick_score = jax.random.randint(jax.random.fold_in(key, 23), (shards, entries, 2 * stretch_blocks), 0, 1 << 16) * (2 * stretch_blocks) + local_ids[None, None, :]
    pick_score = jnp.where(allowed, pick_score, 1 << 30)
    picked = jnp.argmin(pick_score, axis=2).astype(jnp.int32)
    chosen = jnp.take_along_axis(candidate, picked[:, :, None], axis=2)[:, :, 0]
    named_block = jnp.where(jnp.any(allowed, axis=2), chosen, -1).astype(jnp.int32)
    table = named_block.reshape(shards, 2 * stretch_blocks, LINKS)
    first = table[:, :stretch_blocks].reshape(shards * stretch_blocks, LINKS)
    second = table[::-1, stretch_blocks:].reshape(shards * stretch_blocks, LINKS)
    return jnp.concatenate((first, second), 0).astype(jnp.int32)


def block_levels(key, shape, cuts, least, top_value):
    def one(dim, blocks):
        steps = jax.random.uniform(jax.random.fold_in(jax.random.fold_in(key, 6), dim), (blocks,), jnp.float32, least / len(cuts), top_value / len(cuts))
        return jnp.repeat(jnp.exp(steps), shape[dim] // blocks).reshape((-1,) + (1,) * (len(shape) - dim - 1))

    factor_of = one(*cuts[0])
    for cut in cuts[1:]:
        factor_of = factor_of * one(*cut)
    return factor_of


def centred(stream_key, extent, spread, bound, cuts=(), kind=jnp.bfloat16):
    values = jax.random.normal(stream_key, extent, jnp.float32) * spread
    if len(cuts) > 0:
        values = block_levels(stream_key, extent, cuts, -0.22, 0.18) * values
    return jnp.clip(values, min=-bound, max=bound).astype(kind)


def setup_inputs(seed: int = 0) -> dict:
    streams_of = jax.random.split(jax.random.key(seed), 6)
    query = draw_query(jax.random.fold_in(streams_of[5], 71), 0)
    key = draw_key(jax.random.fold_in(streams_of[5], 71), 0)
    value = centred(streams_of[2], (SEQ, WIDTH), 1.0, 6.0, ((0, 8), (1, 4)))
    out_grad = centred(streams_of[3], (SEQ, WIDTH), 1.0, 6.0, ((0, 8), (1, 4)))
    links = draw_links(jax.random.fold_in(streams_of[5], 71), 0)
    return dict(query=query, key=key, value=value, out_grad=out_grad, links=links)


NEG_FILL = -1.0e30


def to_natural(stored):
    half_rows = TOK_DEV // 2
    width = stored.shape[-1]
    parts = stored.reshape(N_CTX, 2, half_rows, width)
    return jnp.concatenate((parts[:, 0].reshape(-1, width), parts[::-1, 1].reshape(-1, width)), 0)


def to_storage(natural):
    half_rows = TOK_DEV // 2
    width = natural.shape[-1]
    first = natural[: N_CTX * half_rows].reshape(N_CTX, half_rows, width)
    second = natural[N_CTX * half_rows:].reshape(N_CTX, half_rows, width)[::-1]
    return jnp.stack((first, second), 1).reshape(-1, width)


def rounded(values):
    return lax.optimization_barrier(values.astype(jnp.bfloat16)).astype(jnp.float32)


def reference(query, key, value, out_grad, links):
    scaling = HEAD_DIM ** -0.5
    span = WIN + LINKS

    def blocked(stored):
        return to_natural(stored).reshape(NBLK, BLK, HEADS, HEAD_DIM)

    q_all = blocked(query)
    k_all = blocked(key)
    v_all = blocked(value)
    o_all = blocked(out_grad)
    offsets = jnp.arange(WIN, dtype=jnp.int32)
    positions = jnp.arange(BLK, dtype=jnp.int32)
    causal = positions[:, None] >= positions[None, :]
    first_only = (jnp.arange(span, dtype=jnp.int32) == 0)[:, None, None]
    inner = jnp.where(first_only, causal[None], True)
    is_link = (jnp.arange(span, dtype=jnp.int32) >= WIN)[:, None, None, None]

    def step(carry, block):
        key_acc, value_acc = carry
        listed = jnp.concatenate((block - offsets, links[block].astype(jnp.int32))).astype(jnp.int32)
        usable = listed >= 0
        safe = jnp.maximum(listed, 0).astype(jnp.int32)
        keys = k_all[safe].astype(jnp.float32)
        values = v_all[safe].astype(jnp.float32)
        q_blk = q_all[block].astype(jnp.float32)
        o_blk = o_all[block].astype(jnp.float32)
        live = (usable[:, None, None] & inner).transpose(1, 0, 2)[None]
        score = jnp.einsum("qhd,skhd->hqsk", q_blk, keys) * scaling
        score = jnp.where(live, score, NEG_FILL)
        top = jnp.max(score, axis=(2, 3), keepdims=True)
        prob = jnp.where(live, jnp.exp(score - top), 0.0)
        prob = prob / jnp.sum(prob, axis=(2, 3), keepdims=True)
        dprob = jnp.einsum("qhd,skhd->hqsk", o_blk, values)
        delta = jnp.sum(prob * dprob, axis=(2, 3), keepdims=True)
        dscore = prob * (dprob - delta)
        prob_b = rounded(prob)
        dscore_b = rounded(dscore)
        dq_window = jnp.einsum("hqsk,skhd->qhd", dscore_b[:, :, :WIN], keys[:WIN]) * scaling
        dq_link = rounded(jnp.einsum("hqsk,skhd->sqhd", dscore_b[:, :, WIN:], keys[WIN:]) * scaling)
        dq_block = dq_window + jnp.sum(dq_link, axis=0)
        dk_terms = jnp.einsum("hqsk,qhd->skhd", dscore_b, q_blk) * scaling
        dv_terms = jnp.einsum("hqsk,qhd->skhd", prob_b, o_blk)
        dk_terms = jnp.where(is_link, rounded(dk_terms), dk_terms)
        dv_terms = jnp.where(is_link, rounded(dv_terms), dv_terms)
        return (key_acc.at[safe].add(dk_terms), value_acc.at[safe].add(dv_terms)), dq_block.astype(jnp.bfloat16)

    zeros_acc = jnp.zeros((NBLK, BLK, HEADS, HEAD_DIM), jnp.float32)
    (key_acc, value_acc), dq_all = lax.scan(step, (zeros_acc, zeros_acc), jnp.arange(NBLK, dtype=jnp.int32))
    rows_all = NBLK * BLK
    query_grad = to_storage(dq_all.reshape(rows_all, HEADS * HEAD_DIM))
    key_grad = to_storage(key_acc.reshape(rows_all, HEADS * HEAD_DIM)).astype(jnp.bfloat16)
    value_grad = to_storage(value_acc.reshape(rows_all, HEADS * HEAD_DIM)).astype(jnp.bfloat16)
    return query_grad, key_grad, value_grad
```

```python
import functools
import math

import jax
import jax.numpy as jnp
from jax import lax
from jax.experimental import pallas as pl
from jax.experimental.pallas import tpu as pltpu
from jax.sharding import PartitionSpec as P

HEAD_DIM = 128
BLK = 128
WIN = 2
LINKS = 6
SPAN = WIN + LINKS
NEG_FILL = -1e30
VMEM_LIMIT = 48 * 1024 * 1024


def swapped(x, by):
    count = lax.axis_size("ctx")
    return lax.ppermute(x, "ctx", [(i, i ^ by) for i in range(count)])


def split_heads_kernel(members, groups, *refs):
    first, second = refs[:2]
    outs = refs[2 : 2 + groups]
    sems = refs[2 + groups]
    chip = lax.axis_index("ctx") // members
    copies = []
    for s in range(groups):
        column = pl.multiple_of((chip ^ s) * HEAD_DIM, HEAD_DIM)
        for t, source in enumerate((first, second)):
            copies.append(
                pltpu.make_async_copy(
                    source.at[:, pl.ds(column, HEAD_DIM)], outs[s].at[t], sems.at[2 * s + t]
                )
            )
    for copy in copies:
        copy.start()
    for copy in copies:
        copy.wait()


def split_heads(first, second, members, groups):
    rows = first.shape[0]
    return pl.pallas_call(
        functools.partial(split_heads_kernel, members, groups),
        out_shape=[jax.ShapeDtypeStruct((2, rows, HEAD_DIM), first.dtype)] * groups,
        in_specs=[pl.BlockSpec(memory_space=pl.ANY)] * 2,
        out_specs=[pl.BlockSpec(memory_space=pl.ANY)] * groups,
        scratch_shapes=[pltpu.SemaphoreType.DMA((2 * groups,))],
        cost_estimate=pl.CostEstimate(
            flops=0, bytes_accessed=4 * first.size * first.dtype.itemsize, transcendentals=0
        ),
        name="split_heads",
    )(first, second)


def join_heads_kernel(members, groups, *refs):
    dq_parts = refs[:groups]
    pair_parts = refs[groups : 2 * groups]
    outs = refs[2 * groups : 2 * groups + 3]
    sems = refs[2 * groups + 3]
    chip = lax.axis_index("ctx") // members
    copies = []
    for s in range(groups):
        column = pl.multiple_of((chip ^ s) * HEAD_DIM, HEAD_DIM)
        for t, source in enumerate((dq_parts[s], pair_parts[s].at[0], pair_parts[s].at[1])):
            copies.append(
                pltpu.make_async_copy(
                    source, outs[t].at[:, pl.ds(column, HEAD_DIM)], sems.at[3 * s + t]
                )
            )
    for copy in copies:
        copy.start()
    for copy in copies:
        copy.wait()


def join_heads(dq_parts, pair_parts, members, groups):
    rows = dq_parts[0].shape[0]
    out = jax.ShapeDtypeStruct((rows, groups * HEAD_DIM), jnp.bfloat16)
    return pl.pallas_call(
        functools.partial(join_heads_kernel, members, groups),
        out_shape=[out] * 3,
        in_specs=[pl.BlockSpec(memory_space=pl.ANY)] * (2 * groups),
        out_specs=[pl.BlockSpec(memory_space=pl.ANY)] * 3,
        scratch_shapes=[pltpu.SemaphoreType.DMA((3 * groups,))],
        cost_estimate=pl.CostEstimate(
            flops=0, bytes_accessed=12 * rows * groups * HEAD_DIM, transcendentals=0
        ),
        name="join_heads",
    )(*dq_parts, *pair_parts)


def dot(left, right, dims):
    return lax.dot_general(left, right, (dims, ((), ())), preferred_element_type=jnp.float32)


def attend_kernel(shards, members, groups, rows, *refs):
    slots = members * groups
    links = refs[0]
    pairs = refs[1 : 1 + slots]
    asks = refs[1 + slots : 1 + slots + groups]
    refs = refs[1 + slots + groups :]
    dq_outs = refs[:groups]
    own_outs = refs[groups : 2 * groups]
    far_outs = refs[2 * groups : 2 * groups + members - 1]
    key_buf, value_buf, query_buf, grad_buf, key_acc, value_acc, sems = refs[
        2 * groups + members - 1 :
    ]
    device = lax.axis_index("ctx")
    local_blocks = rows // BLK
    stretch = local_blocks // 2
    copies = []
    for i in range(slots):
        place = pl.ds(i * rows, rows)
        copies.append(pltpu.make_async_copy(pairs[i].at[0], key_buf.at[place], sems.at[2 * i]))
        copies.append(
            pltpu.make_async_copy(pairs[i].at[1], value_buf.at[place], sems.at[2 * i + 1])
        )
    for s in range(groups):
        place = pl.ds(s * rows, rows)
        at = 2 * (slots + s)
        copies.append(pltpu.make_async_copy(asks[s].at[0], query_buf.at[place], sems.at[at]))
        copies.append(pltpu.make_async_copy(asks[s].at[1], grad_buf.at[place], sems.at[at + 1]))
    for copy in copies:
        copy.start()
    key_acc[...] = jnp.zeros_like(key_acc)
    value_acc[...] = jnp.zeros_like(value_acc)
    for copy in copies:
        copy.wait()

    scaling = HEAD_DIM**-0.5
    causal = lax.broadcasted_iota(jnp.int32, (BLK, BLK), 0) <= lax.broadcasted_iota(
        jnp.int32, (BLK, BLK), 1
    )

    def place_of(block):
        run = lax.div(block, stretch)
        late = run >= shards
        owner = jnp.where(late, 2 * shards - 1 - run, run)
        local = block - run * stretch + jnp.where(late, stretch, 0)
        apart = owner ^ device
        slot = lax.rem(apart, members) * groups + lax.div(apart, members)
        return pl.multiple_of((slot * local_blocks + local) * BLK, BLK)

    for s in range(groups):
        asker = device ^ (s * members)

        def step(local, _, s=s, asker=asker):
            early = asker * stretch + local
            block = jnp.where(
                local < stretch, early, (2 * shards - 1 - asker) * stretch + local - stretch
            )
            listed = [block, block - 1] + [links[block, i] for i in range(LINKS)]
            places = [place_of(jnp.maximum(j, 0)) for j in listed]
            here = pl.ds(pl.multiple_of(s * rows + local * BLK, BLK), BLK)
            q = query_buf[here, :]
            o = grad_buf[here, :]
            keys = jnp.concatenate([key_buf[pl.ds(p, BLK), :] for p in places], 0)
            values = jnp.concatenate([value_buf[pl.ds(p, BLK), :] for p in places], 0)
            raw = dot(keys, q, ((1,), (1,))).reshape(SPAN, BLK, BLK) * (
                scaling * math.log2(math.e)
            )
            parts = [jnp.where(causal, raw[0], NEG_FILL)]
            for i in range(1, SPAN):
                parts.append(raw[i] + jnp.where(listed[i] >= 0, 0.0, NEG_FILL))
            score = jnp.concatenate(parts, 0)
            top = jnp.max(score, axis=0, keepdims=True)
            prob = jnp.exp2(score - top)
            prob = prob * (1.0 / jnp.sum(prob, axis=0, keepdims=True))
            dprob = dot(values, o, ((1,), (1,)))
            delta = jnp.sum(prob * dprob, axis=0, keepdims=True)
            dscore = (prob * (dprob - delta)).astype(jnp.bfloat16)
            prob = prob.astype(jnp.bfloat16)
            dk = dot(dscore, q, ((1,), (0,)))
            dv = dot(prob, o, ((1,), (0,)))
            for i, p in enumerate(places):
                key_acc[pl.ds(p, BLK), :] += dk[i * BLK : (i + 1) * BLK]
                value_acc[pl.ds(p, BLK), :] += dv[i * BLK : (i + 1) * BLK]
            dq = dot(dscore, keys, ((0,), (0,))) * scaling
            dq_outs[s][pl.ds(pl.multiple_of(local * BLK, BLK), BLK), :] = dq.astype(jnp.bfloat16)
            return 0

        lax.fori_loop(0, local_blocks, step, 0)

    for s in range(groups):
        own_outs[s][0] = key_acc[s * rows : (s + 1) * rows, :] * scaling
        own_outs[s][1] = value_acc[s * rows : (s + 1) * rows, :]
    for r in range(1, members):
        for s in range(groups):
            at = slice((r * groups + s) * rows, (r * groups + s + 1) * rows)
            far_outs[r - 1][s, 0] = (key_acc[at, :] * scaling).astype(jnp.bfloat16)
            far_outs[r - 1][s, 1] = value_acc[at, :].astype(jnp.bfloat16)


def attend(links, pairs, asks, shards, members, groups):
    rows = asks[0].shape[1]
    slots = members * groups
    total = slots * rows
    blocks = groups * rows // BLK
    hbm = pl.BlockSpec(memory_space=pl.ANY)
    outs = (
        [jax.ShapeDtypeStruct((rows, HEAD_DIM), jnp.bfloat16)] * groups
        + [jax.ShapeDtypeStruct((2, rows, HEAD_DIM), jnp.float32)] * groups
        + [jax.ShapeDtypeStruct((groups, 2, rows, HEAD_DIM), jnp.bfloat16)] * (members - 1)
    )
    found = pl.pallas_call(
        functools.partial(attend_kernel, shards, members, groups, rows),
        out_shape=outs,
        in_specs=[pl.BlockSpec(memory_space=pltpu.SMEM)] + [hbm] * (slots + groups),
        out_specs=[pl.BlockSpec(memory_space=pltpu.VMEM)] * len(outs),
        scratch_shapes=[
            pltpu.VMEM((total, HEAD_DIM), jnp.bfloat16),
            pltpu.VMEM((total, HEAD_DIM), jnp.bfloat16),
            pltpu.VMEM((groups * rows, HEAD_DIM), jnp.bfloat16),
            pltpu.VMEM((groups * rows, HEAD_DIM), jnp.bfloat16),
            pltpu.VMEM((total, HEAD_DIM), jnp.float32),
            pltpu.VMEM((total, HEAD_DIM), jnp.float32),
            pltpu.SemaphoreType.DMA((2 * (slots + groups),)),
        ],
        compiler_params=pltpu.CompilerParams(vmem_limit_bytes=VMEM_LIMIT),
        cost_estimate=pl.CostEstimate(
            flops=10 * blocks * SPAN * BLK * BLK * HEAD_DIM,
            bytes_accessed=8 * total * HEAD_DIM,
            transcendentals=blocks * SPAN * BLK * BLK,
        ),
        name="attend",
    )(links, *pairs, *asks)
    return found[:groups], found[groups : 2 * groups], found[2 * groups :]


def per_device(query, key, value, out_grad, links):
    groups = query.shape[1] // HEAD_DIM
    shards = lax.axis_size("ctx")
    members = shards // groups

    pairs = split_heads(key, value, members, groups)
    asks = split_heads(query, out_grad, members, groups)
    pairs = [pairs[0]] + [swapped(pairs[s], s * members) for s in range(1, groups)]
    asks = [asks[0]] + [swapped(asks[s], s * members) for s in range(1, groups)]
    pairs = pairs + [swapped(pairs[s], r) for r in range(1, members) for s in range(groups)]

    dq_parts, own, far = attend(links, pairs, asks, shards, members, groups)

    dq_parts = [dq_parts[0]] + [swapped(dq_parts[s], s * members) for s in range(1, groups)]
    far = [swapped(far[r - 1], r) for r in range(1, members)]
    pair_parts = []
    for s in range(groups):
        total = own[s]
        for part in far:
            total = total + part[s].astype(jnp.float32)
        total = total.astype(jnp.bfloat16)
        pair_parts.append(total if s == 0 else swapped(total, s * members))
    return tuple(join_heads(dq_parts, pair_parts, members, groups))


def solution(mesh):
    return jax.shard_map(
        per_device,
        mesh=mesh,
        in_specs=(P("ctx", "head"), P("ctx", "head"), P("ctx", "head"), P("ctx", "head"), P()),
        out_specs=(P("ctx", "head"), P("ctx", "head"), P("ctx", "head")),
        check_vma=False,
    )
```

```python
import functools
import math

import jax
import jax.numpy as jnp
from jax import lax
from jax.experimental import pallas as pl
from jax.experimental.pallas import tpu as pltpu
from jax.sharding import PartitionSpec as P

HEAD_DIM = 128
BLK = 128
WIN = 2
LINKS = 6
SPAN = WIN + LINKS
NEG_FILL = -1e30
VMEM_LIMIT = 48 * 1024 * 1024


def swapped(x, by):
    count = lax.axis_size("ctx")
    return lax.ppermute(x, "ctx", [(i, i ^ by) for i in range(count)])


def split_heads_kernel(members, groups, *refs):
    first, second = refs[:2]
    outs = refs[2:]
    chip = lax.axis_index("ctx") // members
    for s in range(groups):
        column = pl.ds(pl.multiple_of((chip ^ s) * HEAD_DIM, HEAD_DIM), HEAD_DIM)
        outs[s][0] = first[:, column]
        outs[s][1] = second[:, column]


def split_heads(first, second, members, groups):
    rows = first.shape[0]
    vmem = pl.BlockSpec(memory_space=pltpu.VMEM)
    return pl.pallas_call(
        functools.partial(split_heads_kernel, members, groups),
        out_shape=[jax.ShapeDtypeStruct((2, rows, HEAD_DIM), first.dtype)] * groups,
        in_specs=[vmem] * 2,
        out_specs=[vmem] * groups,
        compiler_params=pltpu.CompilerParams(vmem_limit_bytes=VMEM_LIMIT),
        cost_estimate=pl.CostEstimate(
            flops=0, bytes_accessed=4 * first.size * first.dtype.itemsize, transcendentals=0
        ),
        name="split_heads",
    )(first, second)


def join_heads_kernel(members, groups, *refs):
    dq_parts = refs[:groups]
    pair_parts = refs[groups : 2 * groups]
    outs = refs[2 * groups :]
    chip = lax.axis_index("ctx") // members
    for s in range(groups):
        column = pl.ds(pl.multiple_of((chip ^ s) * HEAD_DIM, HEAD_DIM), HEAD_DIM)
        outs[0][:, column] = dq_parts[s][...]
        outs[1][:, column] = pair_parts[s][0]
        outs[2][:, column] = pair_parts[s][1]


def join_heads(dq_parts, pair_parts, members, groups):
    rows = dq_parts[0].shape[0]
    vmem = pl.BlockSpec(memory_space=pltpu.VMEM)
    out = jax.ShapeDtypeStruct((rows, groups * HEAD_DIM), jnp.bfloat16)
    return pl.pallas_call(
        functools.partial(join_heads_kernel, members, groups),
        out_shape=[out] * 3,
        in_specs=[vmem] * (2 * groups),
        out_specs=[vmem] * 3,
        compiler_params=pltpu.CompilerParams(vmem_limit_bytes=VMEM_LIMIT),
        cost_estimate=pl.CostEstimate(
            flops=0, bytes_accessed=12 * rows * groups * HEAD_DIM, transcendentals=0
        ),
        name="join_heads",
    )(*dq_parts, *pair_parts)


def dot(left, right, dims):
    return lax.dot_general(left, right, (dims, ((), ())), preferred_element_type=jnp.float32)


def attend_kernel(shards, members, groups, rows, *refs):
    slots = members * groups
    links = refs[0]
    pairs = refs[1 : 1 + slots]
    asks = refs[1 + slots : 1 + slots + groups]
    refs = refs[1 + slots + groups :]
    dq_outs = refs[:groups]
    own_outs = refs[groups : 2 * groups]
    far_outs = refs[2 * groups : 2 * groups + members - 1]
    key_buf, value_buf, query_buf, grad_buf, key_acc, value_acc, sems = refs[
        2 * groups + members - 1 :
    ]
    device = lax.axis_index("ctx")
    local_blocks = rows // BLK
    stretch = local_blocks // 2
    copies = []
    for i in range(slots):
        place = pl.ds(i * rows, rows)
        copies.append(pltpu.make_async_copy(pairs[i].at[0], key_buf.at[place], sems.at[2 * i]))
        copies.append(
            pltpu.make_async_copy(pairs[i].at[1], value_buf.at[place], sems.at[2 * i + 1])
        )
    for s in range(groups):
        place = pl.ds(s * rows, rows)
        at = 2 * (slots + s)
        copies.append(pltpu.make_async_copy(asks[s].at[0], query_buf.at[place], sems.at[at]))
        copies.append(pltpu.make_async_copy(asks[s].at[1], grad_buf.at[place], sems.at[at + 1]))
    for copy in copies:
        copy.start()
    key_acc[...] = jnp.zeros_like(key_acc)
    value_acc[...] = jnp.zeros_like(value_acc)
    for copy in copies:
        copy.wait()

    scaling = HEAD_DIM**-0.5
    causal = lax.broadcasted_iota(jnp.int32, (BLK, BLK), 0) <= lax.broadcasted_iota(
        jnp.int32, (BLK, BLK), 1
    )

    def place_of(block):
        run = lax.div(block, stretch)
        late = run >= shards
        owner = jnp.where(late, 2 * shards - 1 - run, run)
        local = block - run * stretch + jnp.where(late, stretch, 0)
        apart = owner ^ device
        slot = lax.rem(apart, members) * groups + lax.div(apart, members)
        return pl.multiple_of((slot * local_blocks + local) * BLK, BLK)

    for s in range(groups):
        asker = device ^ (s * members)

        def step(local, _, s=s, asker=asker):
            early = asker * stretch + local
            block = jnp.where(
                local < stretch, early, (2 * shards - 1 - asker) * stretch + local - stretch
            )
            listed = [block, block - 1] + [links[block, i] for i in range(LINKS)]
            places = [place_of(jnp.maximum(j, 0)) for j in listed]
            here = pl.ds(pl.multiple_of(s * rows + local * BLK, BLK), BLK)
            q = query_buf[here, :]
            o = grad_buf[here, :]
            keys = jnp.concatenate([key_buf[pl.ds(p, BLK), :] for p in places], 0)
            values = jnp.concatenate([value_buf[pl.ds(p, BLK), :] for p in places], 0)
            raw = dot(keys, q, ((1,), (1,))).reshape(SPAN, BLK, BLK) * (
                scaling * math.log2(math.e)
            )
            parts = [jnp.where(causal, raw[0], NEG_FILL)]
            for i in range(1, SPAN):
                parts.append(raw[i] + jnp.where(listed[i] >= 0, 0.0, NEG_FILL))
            score = jnp.concatenate(parts, 0)
            top = jnp.max(score, axis=0, keepdims=True)
            prob = jnp.exp2(score - top)
            prob = prob * (1.0 / jnp.sum(prob, axis=0, keepdims=True))
            dprob = dot(values, o, ((1,), (1,)))
            delta = jnp.sum(prob * dprob, axis=0, keepdims=True)
            dscore = (prob * (dprob - delta)).astype(jnp.bfloat16)
            prob = prob.astype(jnp.bfloat16)
            dk = dot(dscore, q, ((1,), (0,)))
            dv = dot(prob, o, ((1,), (0,)))
            for i, p in enumerate(places):
                key_acc[pl.ds(p, BLK), :] += dk[i * BLK : (i + 1) * BLK]
                value_acc[pl.ds(p, BLK), :] += dv[i * BLK : (i + 1) * BLK]
            dq = dot(dscore, keys, ((0,), (0,))) * scaling
            dq_outs[s][pl.ds(pl.multiple_of(local * BLK, BLK), BLK), :] = dq.astype(jnp.bfloat16)
            return 0

        lax.fori_loop(0, local_blocks, step, 0)

    for s in range(groups):
        own_outs[s][0] = key_acc[s * rows : (s + 1) * rows, :] * scaling
        own_outs[s][1] = value_acc[s * rows : (s + 1) * rows, :]
    for r in range(1, members):
        for s in range(groups):
            at = slice((r * groups + s) * rows, (r * groups + s + 1) * rows)
            far_outs[r - 1][s, 0] = (key_acc[at, :] * scaling).astype(jnp.bfloat16)
            far_outs[r - 1][s, 1] = value_acc[at, :].astype(jnp.bfloat16)


def attend(links, pairs, asks, shards, members, groups):
    rows = asks[0].shape[1]
    slots = members * groups
    total = slots * rows
    blocks = groups * rows // BLK
    hbm = pl.BlockSpec(memory_space=pl.ANY)
    outs = (
        [jax.ShapeDtypeStruct((rows, HEAD_DIM), jnp.bfloat16)] * groups
        + [jax.ShapeDtypeStruct((2, rows, HEAD_DIM), jnp.float32)] * groups
        + [jax.ShapeDtypeStruct((groups, 2, rows, HEAD_DIM), jnp.bfloat16)] * (members - 1)
    )
    found = pl.pallas_call(
        functools.partial(attend_kernel, shards, members, groups, rows),
        out_shape=outs,
        in_specs=[pl.BlockSpec(memory_space=pltpu.SMEM)] + [hbm] * (slots + groups),
        out_specs=[pl.BlockSpec(memory_space=pltpu.VMEM)] * len(outs),
        scratch_shapes=[
            pltpu.VMEM((total, HEAD_DIM), jnp.bfloat16),
            pltpu.VMEM((total, HEAD_DIM), jnp.bfloat16),
            pltpu.VMEM((groups * rows, HEAD_DIM), jnp.bfloat16),
            pltpu.VMEM((groups * rows, HEAD_DIM), jnp.bfloat16),
            pltpu.VMEM((total, HEAD_DIM), jnp.float32),
            pltpu.VMEM((total, HEAD_DIM), jnp.float32),
            pltpu.SemaphoreType.DMA((2 * (slots + groups),)),
        ],
        compiler_params=pltpu.CompilerParams(vmem_limit_bytes=VMEM_LIMIT),
        cost_estimate=pl.CostEstimate(
            flops=10 * blocks * SPAN * BLK * BLK * HEAD_DIM,
            bytes_accessed=8 * total * HEAD_DIM,
            transcendentals=blocks * SPAN * BLK * BLK,
        ),
        name="attend",
    )(links, *pairs, *asks)
    return found[:groups], found[groups : 2 * groups], found[2 * groups :]


def per_device(query, key, value, out_grad, links):
    groups = query.shape[1] // HEAD_DIM
    shards = lax.axis_size("ctx")
    members = shards // groups

    pairs = split_heads(key, value, members, groups)
    asks = split_heads(query, out_grad, members, groups)
    pairs = [pairs[0]] + [swapped(pairs[s], s * members) for s in range(1, groups)]
    asks = [asks[0]] + [swapped(asks[s], s * members) for s in range(1, groups)]
    pairs = pairs + [swapped(pairs[s], r) for r in range(1, members) for s in range(groups)]

    dq_parts, own, far = attend(links, pairs, asks, shards, members, groups)

    dq_parts = [dq_parts[0]] + [swapped(dq_parts[s], s * members) for s in range(1, groups)]
    far = [swapped(far[r - 1], r) for r in range(1, members)]
    pair_parts = []
    for s in range(groups):
        total = own[s]
        for part in far:
            total = total + part[s].astype(jnp.float32)
        total = total.astype(jnp.bfloat16)
        pair_parts.append(total if s == 0 else swapped(total, s * members))
    return tuple(join_heads(dq_parts, pair_parts, members, groups))


def solution(mesh):
    return jax.shard_map(
        per_device,
        mesh=mesh,
        in_specs=(P("ctx", "head"), P("ctx", "head"), P("ctx", "head"), P("ctx", "head"), P()),
        out_specs=(P("ctx", "head"), P("ctx", "head"), P("ctx", "head")),
        check_vma=False,
    )
```

```python
import functools
import math

import jax
import jax.numpy as jnp
from jax import lax
from jax.experimental import pallas as pl
from jax.experimental.pallas import tpu as pltpu
from jax.sharding import PartitionSpec as P

HEAD_DIM = 128
BLK = 128
WIN = 2
LINKS = 6
SPAN = WIN + LINKS
NEG_FILL = -1e30
VMEM_LIMIT = 24 * 1024 * 1024
FAR_LIMIT = 40 * 1024 * 1024
SPLIT_LIMIT = 56 * 1024 * 1024
SMALL_LIMIT = 16 * 1024 * 1024


def swapped(x, by):
    count = lax.axis_size("ctx")
    return lax.ppermute(x, "ctx", [(i, i ^ by) for i in range(count)])


def chip_column(members, s):
    chip = lax.div(lax.axis_index("ctx"), members)
    return pl.ds(pl.multiple_of((chip ^ s) * HEAD_DIM, HEAD_DIM), HEAD_DIM)


def all_started(moves, sems):
    copies = [
        pltpu.make_async_copy(source, target, sems.at[i])
        for i, (source, target) in enumerate(moves)
    ]
    for copy in copies:
        copy.start()
    return copies


def split_heads_kernel(which, members, groups, *refs):
    query, key, value, grad = refs[:4]
    outs = refs[4:-1]
    half = query.shape[0] // 2
    taken = pl.ds(which * half, half)
    moves = []
    for s in range(groups):
        column = chip_column(members, s)
        for t, (pair, ask) in enumerate(((key, query), (value, grad))):
            lanes = pl.ds(t * HEAD_DIM, HEAD_DIM)
            moves.append((pair.at[taken, column], outs[s].at[pl.ds(0, half), lanes]))
            moves.append((ask.at[taken, column], outs[s].at[pl.ds(half, half), lanes]))
    for copy in all_started(moves, refs[-1]):
        copy.wait()


def split_heads(which, arrays, members, groups):
    rows = arrays[0].shape[0]
    out = jax.ShapeDtypeStruct((rows, 2 * HEAD_DIM), jnp.bfloat16)
    return pl.pallas_call(
        functools.partial(split_heads_kernel, which, members, groups),
        out_shape=[out] * groups,
        in_specs=[pl.BlockSpec(memory_space=pl.ANY)] * len(arrays),
        out_specs=[pl.BlockSpec(memory_space=pltpu.VMEM)] * groups,
        scratch_shapes=[pltpu.SemaphoreType.DMA((4 * groups,))],
        compiler_params=pltpu.CompilerParams(vmem_limit_bytes=SPLIT_LIMIT),
        cost_estimate=pl.CostEstimate(
            flops=0, bytes_accessed=8 * groups * rows * HEAD_DIM, transcendentals=0
        ),
        name="split_late" if which else "split_early",
    )(*arrays)


def join_heads_kernel(members, groups, *refs):
    parts = refs[:groups]
    outs = refs[groups:]
    rows = outs[0].shape[0]
    for s in range(groups):
        column = chip_column(members, s)
        for n in range(rows // BLK):
            at = slice(n * BLK, (n + 1) * BLK)
            packed = rows + n // 2 * BLK
            lanes = slice(n % 2 * HEAD_DIM, (n % 2 + 1) * HEAD_DIM)
            outs[0][at, column] = parts[s][packed : packed + BLK, lanes]
            outs[1][at, column] = parts[s][at, :HEAD_DIM]
            outs[2][at, column] = parts[s][at, HEAD_DIM:]


def join_heads(parts, rows, members, groups):
    vmem = pl.BlockSpec(memory_space=pltpu.VMEM)
    out = jax.ShapeDtypeStruct((rows, groups * HEAD_DIM), jnp.bfloat16)
    return pl.pallas_call(
        functools.partial(join_heads_kernel, members, groups),
        out_shape=[out] * 3,
        in_specs=[vmem] * groups,
        out_specs=[vmem] * 3,
        compiler_params=pltpu.CompilerParams(vmem_limit_bytes=SMALL_LIMIT),
        cost_estimate=pl.CostEstimate(
            flops=0, bytes_accessed=12 * rows * groups * HEAD_DIM, transcendentals=0
        ),
        name="join_heads",
    )(*parts)


def add_kernel(members, groups, *refs):
    far = refs[:  members - 1]
    own, dq_early, dq_late = (
        refs[members - 1 + i * groups : members - 1 + (i + 1) * groups] for i in range(3)
    )
    outs = refs[members - 1 + 3 * groups :]
    rows = own[0].shape[0]
    quarter = rows // 4
    for s in range(groups):
        total = own[s][...].astype(jnp.float32)
        for part in far:
            total = total + part[s].astype(jnp.float32)
        outs[s][:rows, :HEAD_DIM] = (total[:, :HEAD_DIM] * HEAD_DIM**-0.5).astype(jnp.bfloat16)
        outs[s][:rows, HEAD_DIM:] = total[:, HEAD_DIM:].astype(jnp.bfloat16)
        outs[s][rows : rows + quarter] = dq_early[s][...]
        outs[s][rows + quarter :] = dq_late[s][...]


def add_partials(far, own, dq_early, dq_late, members, groups):
    vmem = pl.BlockSpec(memory_space=pltpu.VMEM)
    rows = own[0].shape[0]
    out = jax.ShapeDtypeStruct((rows + rows // 2, 2 * HEAD_DIM), jnp.bfloat16)
    given = [*far, *own, *dq_early, *dq_late]
    return pl.pallas_call(
        functools.partial(add_kernel, members, groups),
        out_shape=[out] * groups,
        in_specs=[vmem] * len(given),
        out_specs=[vmem] * groups,
        compiler_params=pltpu.CompilerParams(vmem_limit_bytes=SMALL_LIMIT),
        cost_estimate=pl.CostEstimate(
            flops=0, bytes_accessed=8 * groups * rows * HEAD_DIM, transcendentals=0
        ),
        name="add_partials",
    )(*given)


def dot(left, right, dims):
    return lax.dot_general(left, right, (dims, ((), ())), preferred_element_type=jnp.float32)


def attend_kernel(late, near, shards, members, groups, half, *refs):
    slots = members * groups
    halves = 2 if late else 1
    held = halves * half
    stretch = half // BLK
    links = refs[0]
    packs = [refs[1 + h * slots : 1 + (h + 1) * slots] for h in range(halves)]
    refs = refs[1 + halves * slots :]
    if late:
        sums_in = refs[0]
        refs = refs[1:]
    dq_outs = refs[:groups]
    refs = refs[groups:]
    if late:
        own_outs = refs[:groups]
        far_outs = refs[groups : groups + members - 1]
        pair_buf, ask_buf, dq_buf, sems, acc = refs[groups + members - 1 :]
    else:
        acc, pair_buf, ask_buf, dq_buf, sems = refs
    device = lax.axis_index("ctx")

    moves = []
    for h in range(halves):
        for i in range(slots):
            place = pl.ds(i * held + h * half, half)
            moves.append((packs[h][i].at[pl.ds(0, half)], pair_buf.at[place]))
            if late and h == 0:
                moves.append((sums_in.at[pl.ds(i * half, half)], acc.at[place]))
            else:
                acc[place, :] = jnp.zeros((half, 2 * HEAD_DIM), jnp.float32)
    for s in range(groups):
        place = pl.ds(s * half, half)
        moves.append((packs[-1][s].at[pl.ds(half, half)], ask_buf.at[place]))
    if near:
        for source, target in moves:
            target[...] = source[...]
    else:
        for copy in all_started(moves, sems):
            copy.wait()

    scaling = HEAD_DIM**-0.5
    causal = lax.broadcasted_iota(jnp.int32, (BLK, BLK), 0) <= lax.broadcasted_iota(
        jnp.int32, (BLK, BLK), 1
    )
    blank = jnp.zeros((BLK, HEAD_DIM), jnp.bfloat16)

    def place_of(block):
        run = lax.div(block, stretch)
        local = block - run * stretch
        owner = run
        if late:
            is_late = run >= shards
            owner = jnp.where(is_late, 2 * shards - 1 - run, run)
            local = local + jnp.where(is_late, stretch, 0)
        apart = owner ^ device
        slot = lax.rem(apart, members) * groups + lax.div(apart, members)
        return pl.multiple_of(slot * held + local * BLK, BLK)

    def step(s, _):
        asker = device ^ (s * members)
        first = (2 * shards - 1 - asker if late else asker) * stretch
        units = range(stretch)
        listed = []
        for n in units:
            block = first + n
            listed.append([block, block - 1] + [links[block, i] for i in range(LINKS)])
        places = [[place_of(jnp.maximum(j, 0)) for j in row] for row in listed]
        pairs = [jnp.concatenate([pair_buf[pl.ds(p, BLK), :] for p in row], 0) for row in places]
        wide = []
        for n in units:
            ask = ask_buf[pl.ds(pl.multiple_of(s * half + n * BLK, BLK), BLK), :]
            wide.append(
                jnp.concatenate(
                    [
                        jnp.concatenate([ask[:, :HEAD_DIM], blank], 1),
                        jnp.concatenate([blank, ask[:, HEAD_DIM:]], 1),
                    ],
                    0,
                )
            )
        both = [dot(pairs[n], wide[n], ((1,), (1,))) for n in units]
        dscore_b, terms = [], []
        for n in units:
            raw = [both[n][i * BLK : (i + 1) * BLK, :BLK] for i in range(SPAN)]
            dprob = both[n][:, BLK:].reshape(SPAN, BLK, BLK)
            raw[0] = jnp.where(causal, raw[0], NEG_FILL)
            unused = [0.0] + [jnp.where(j >= 0, 0.0, NEG_FILL) for j in listed[n][1:]]
            tops = [jnp.max(raw[i], axis=0, keepdims=True) + unused[i] for i in range(SPAN)]
            top = functools.reduce(jnp.maximum, tops)
            weight = jnp.stack(
                [
                    jnp.exp2((raw[i] - (top - unused[i])) * (scaling * math.log2(math.e)))
                    for i in range(SPAN)
                ]
            )
            share = 1.0 / jnp.sum(weight, axis=(0, 1), keepdims=True)
            delta = jnp.sum(weight * dprob, axis=(0, 1), keepdims=True) * share
            prob = weight * share
            dscore = (prob * (dprob - delta)).astype(jnp.bfloat16).reshape(SPAN * BLK, BLK)
            dscore_b.append(dscore)
            prob = prob.astype(jnp.bfloat16).reshape(SPAN * BLK, BLK)
            terms.append(dot(jnp.concatenate([dscore, prob], 1), wide[n], ((1,), (0,))))
        dq = [dot(dscore_b[n], pairs[n][:, :HEAD_DIM], ((0,), (0,))) * scaling for n in units]
        for n in units:
            lanes = slice(n % 2 * HEAD_DIM, (n % 2 + 1) * HEAD_DIM)
            packed = pl.ds(pl.multiple_of(s * (half // 2) + n // 2 * BLK, BLK), BLK)
            dq_buf[packed, lanes] = dq[n].astype(jnp.bfloat16)
            for i, p in enumerate(places[n]):
                acc[pl.ds(p, BLK), :] += terms[n][i * BLK : (i + 1) * BLK]
        return 0

    lax.fori_loop(0, groups, step, 0)

    for s in range(groups):
        dq_outs[s][...] = dq_buf[s * (half // 2) : (s + 1) * (half // 2), :]
    if late:
        for s in range(groups):
            own_outs[s][...] = acc[s * held : (s + 1) * held, :].astype(jnp.bfloat16)
        for r in range(1, members):
            for s in range(groups):
                start = (r * groups + s) * held
                far_outs[r - 1][s] = acc[start : start + held, :].astype(jnp.bfloat16)


def attend(links, packs, sums, shards, members, groups):
    late = sums is not None
    half = packs[0][0].shape[0] // 2
    slots = members * groups
    held = half * len(packs)
    blocks = groups * half // BLK
    given = [pack for part in packs for pack in part] + ([sums] if late else [])
    dq = jax.ShapeDtypeStruct((half // 2, 2 * HEAD_DIM), jnp.bfloat16)
    outs = [dq] * groups
    scratch = [
        pltpu.VMEM((slots * held, 2 * HEAD_DIM), jnp.bfloat16),
        pltpu.VMEM((groups * half, 2 * HEAD_DIM), jnp.bfloat16),
        pltpu.VMEM((groups * half // 2, 2 * HEAD_DIM), jnp.bfloat16),
        pltpu.SemaphoreType.DMA((3 * slots + groups,)),
    ]
    if late:
        outs += [jax.ShapeDtypeStruct((held, 2 * HEAD_DIM), jnp.bfloat16)] * groups
        far = jax.ShapeDtypeStruct((groups, held, 2 * HEAD_DIM), jnp.bfloat16)
        outs += [far] * (members - 1)
        scratch += [pltpu.VMEM((slots * held, 2 * HEAD_DIM), jnp.float32)]
    else:
        outs += [jax.ShapeDtypeStruct((slots * held, 2 * HEAD_DIM), jnp.float32)]
    near = slots * half <= 4096
    vmem = pl.BlockSpec(memory_space=pltpu.VMEM)
    found = pl.pallas_call(
        functools.partial(attend_kernel, late, near, shards, members, groups, half),
        out_shape=outs,
        in_specs=[pl.BlockSpec(memory_space=pltpu.SMEM)]
        + [vmem if near else pl.BlockSpec(memory_space=pl.ANY)] * len(given),
        out_specs=[vmem] * len(outs),
        scratch_shapes=scratch,
        compiler_params=pltpu.CompilerParams(vmem_limit_bytes=VMEM_LIMIT if near else FAR_LIMIT),
        cost_estimate=pl.CostEstimate(
            flops=10 * blocks * SPAN * BLK * BLK * HEAD_DIM,
            bytes_accessed=8 * slots * held * HEAD_DIM,
            transcendentals=blocks * SPAN * BLK * BLK,
        ),
        name="attend_late" if late else "attend_early",
    )(links, *given)
    if late:
        return found[:groups], found[groups : 2 * groups], found[2 * groups :]
    return found[:groups], found[groups]


def to_chips(parts, members):
    return [parts[0]] + [swapped(part, s * members) for s, part in enumerate(parts[1:], 1)]


def with_members(parts, members):
    return parts + [swapped(part, r) for r in range(1, members) for part in parts]


def per_device(query, key, value, out_grad, links):
    rows, width = query.shape
    groups = width // HEAD_DIM
    shards = lax.axis_size("ctx")
    members = shards // groups
    arrays = (query, key, value, out_grad)

    early = with_members(to_chips(split_heads(0, arrays, members, groups), members), members)
    late = with_members(to_chips(split_heads(1, arrays, members, groups), members), members)
    dq_early, sums = attend(links, [early], None, shards, members, groups)
    dq_late, own, far = attend(links, [early, late], sums, shards, members, groups)
    far = [swapped(part, r) for r, part in enumerate(far, 1)]
    parts = add_partials(far, own, dq_early, dq_late, members, groups)
    return tuple(join_heads(to_chips(parts, members), rows, members, groups))


def solution(mesh):
    return jax.shard_map(
        per_device,
        mesh=mesh,
        in_specs=(P("ctx", "head"), P("ctx", "head"), P("ctx", "head"), P("ctx", "head"), P()),
        out_specs=(P("ctx", "head"), P("ctx", "head"), P("ctx", "head")),
        check_vma=False,
    )
```

```python
import functools
import math

import jax
import jax.numpy as jnp
from jax import lax
from jax.experimental import pallas as pl
from jax.experimental.pallas import tpu as pltpu
from jax.sharding import PartitionSpec as P

HEAD_DIM = 128
BLK = 128
WIN = 2
LINKS = 6
SPAN = WIN + LINKS
NEG_FILL = -1e30
SPLIT_LIMIT = 56 * 1024 * 1024
SMALL_LIMIT = 16 * 1024 * 1024


def swapped(x, by):
    count = lax.axis_size("ctx")
    return lax.ppermute(x, "ctx", [(i, i ^ by) for i in range(count)])


def chip_column(members, s):
    chip = lax.div(lax.axis_index("ctx"), members)
    return pl.ds(pl.multiple_of((chip ^ s) * HEAD_DIM, HEAD_DIM), HEAD_DIM)


def all_started(moves, sems):
    copies = [
        pltpu.make_async_copy(source, target, sems.at[i])
        for i, (source, target) in enumerate(moves)
    ]
    for copy in copies:
        copy.start()
    return copies


def split_heads_kernel(which, members, groups, *refs):
    query, key, value, grad = refs[:4]
    outs = refs[-1 - groups : -1]
    half = query.shape[0] // 2
    taken = pl.ds(which * half, half)
    moves = []
    for s in range(groups):
        column = chip_column(members, s)
        for t, (pair, ask) in enumerate(((key, query), (value, grad))):
            lanes = pl.ds(t * HEAD_DIM, HEAD_DIM)
            moves.append((pair.at[taken, column], outs[s].at[pl.ds(0, half), lanes]))
            moves.append((ask.at[taken, column], outs[s].at[pl.ds(half, half), lanes]))
    for copy in all_started(moves, refs[-1]):
        copy.wait()


def split_heads(which, arrays, after, members, groups):
    rows = arrays[0].shape[0]
    out = jax.ShapeDtypeStruct((rows, 2 * HEAD_DIM), jnp.bfloat16)
    return pl.pallas_call(
        functools.partial(split_heads_kernel, which, members, groups),
        out_shape=[out] * groups,
        in_specs=[pl.BlockSpec(memory_space=pl.ANY)] * (len(arrays) + len(after)),
        out_specs=[pl.BlockSpec(memory_space=pltpu.VMEM)] * groups,
        scratch_shapes=[pltpu.SemaphoreType.DMA((4 * groups,))],
        compiler_params=pltpu.CompilerParams(vmem_limit_bytes=SPLIT_LIMIT),
        cost_estimate=pl.CostEstimate(
            flops=0, bytes_accessed=8 * groups * rows * HEAD_DIM, transcendentals=0
        ),
        name="split_late" if which else "split_early",
    )(*arrays, *after)


def pairs_kernel(groups, *refs):
    out = refs[-1]
    for s in range(groups):
        out[s] = refs[s][: out.shape[1], :]


def only_pairs(packs, after, groups):
    half = packs[0].shape[0] // 2
    vmem = pl.BlockSpec(memory_space=pltpu.VMEM)
    return pl.pallas_call(
        functools.partial(pairs_kernel, groups),
        out_shape=jax.ShapeDtypeStruct((groups, half, 2 * HEAD_DIM), jnp.bfloat16),
        in_specs=[vmem] * groups + [pl.BlockSpec(memory_space=pl.ANY)] * len(after),
        out_specs=vmem,
        compiler_params=pltpu.CompilerParams(vmem_limit_bytes=SMALL_LIMIT),
        cost_estimate=pl.CostEstimate(
            flops=0, bytes_accessed=8 * groups * half * HEAD_DIM, transcendentals=0
        ),
        name="only_pairs",
    )(*packs, *after)


def join_heads_kernel(members, groups, *refs):
    pairs = refs[:groups]
    dqs = refs[groups : 2 * groups]
    outs = refs[2 * groups :]
    for s in range(groups):
        column = chip_column(members, s)
        outs[1][:, column] = pairs[s][:, :HEAD_DIM]
        outs[2][:, column] = pairs[s][:, HEAD_DIM:]
        for n in range(outs[0].shape[0] // BLK):
            packed = slice(n // 2 * BLK, (n // 2 + 1) * BLK)
            lanes = slice(n % 2 * HEAD_DIM, (n % 2 + 1) * HEAD_DIM)
            outs[0][n * BLK : (n + 1) * BLK, column] = dqs[s][packed, lanes]


def join_heads(dqs, pairs, members, groups):
    rows = pairs[0].shape[0]
    vmem = pl.BlockSpec(memory_space=pltpu.VMEM)
    out = jax.ShapeDtypeStruct((rows, groups * HEAD_DIM), jnp.bfloat16)
    return pl.pallas_call(
        functools.partial(join_heads_kernel, members, groups),
        out_shape=[out] * 3,
        in_specs=[vmem] * (2 * groups),
        out_specs=[vmem] * 3,
        compiler_params=pltpu.CompilerParams(vmem_limit_bytes=SMALL_LIMIT),
        cost_estimate=pl.CostEstimate(
            flops=0, bytes_accessed=12 * rows * groups * HEAD_DIM, transcendentals=0
        ),
        name="join_heads",
    )(*pairs, *dqs)


def add_kernel(members, groups, *refs):
    far = refs[: members - 1]
    own = refs[members - 1 : members - 1 + groups]
    outs = refs[members - 1 + groups :]
    for s in range(groups):
        total = own[s][...].astype(jnp.float32)
        for part in far:
            total = total + part[s].astype(jnp.float32)
        outs[s][:, :HEAD_DIM] = (total[:, :HEAD_DIM] * HEAD_DIM**-0.5).astype(jnp.bfloat16)
        outs[s][:, HEAD_DIM:] = total[:, HEAD_DIM:].astype(jnp.bfloat16)


def add_partials(far, own, members, groups):
    vmem = pl.BlockSpec(memory_space=pltpu.VMEM)
    out = jax.ShapeDtypeStruct(own[0].shape, jnp.bfloat16)
    return pl.pallas_call(
        functools.partial(add_kernel, members, groups),
        out_shape=[out] * groups,
        in_specs=[vmem] * (members - 1 + groups),
        out_specs=[vmem] * groups,
        compiler_params=pltpu.CompilerParams(vmem_limit_bytes=SMALL_LIMIT),
        cost_estimate=pl.CostEstimate(
            flops=0, bytes_accessed=8 * groups * own[0].size, transcendentals=0
        ),
        name="add_partials",
    )(*far, *own)


def dot(left, right, dims):
    return lax.dot_general(left, right, (dims, ((), ())), preferred_element_type=jnp.float32)


def attend_kernel(late, near, shards, members, groups, half, *refs):
    slots = members * groups
    rows = 2 * half
    stretch = half // BLK
    links = refs[0]
    refs = refs[1:]
    if late:
        packs = [*refs[:groups]]
        for part in refs[groups : groups + members - 1]:
            packs += [part.at[s] for s in range(groups)]
        dq_early = refs[groups + members - 1 : 2 * groups + members - 1]
        refs = refs[2 * groups + members + 1 :]
        dq_outs = refs[:groups]
        own_outs = refs[groups : 2 * groups]
        far_outs = refs[2 * groups : 2 * groups + members - 1]
        refs = refs[2 * groups + members - 1 :]
    else:
        packs = refs[:slots]
        dq_outs = refs[slots : slots + groups]
        refs = refs[slots + groups :]
    pair_buf, acc, ask_buf, dq_buf, sems = refs
    device = lax.axis_index("ctx")

    moves = []
    for i in range(slots):
        place = pl.ds(i * rows + (half if late else 0), half)
        moves.append((packs[i].at[pl.ds(0, half)], pair_buf.at[place]))
    for s in range(groups):
        moves.append((packs[s].at[pl.ds(half, half)], ask_buf.at[pl.ds(s * half, half)]))
    if near:
        for source, target in moves:
            target[...] = source[...]
    else:
        copies = all_started(moves, sems)
    if not late:
        acc[...] = jnp.zeros_like(acc)
    if not near:
        for copy in copies:
            copy.wait()

    scaling = HEAD_DIM**-0.5
    causal = lax.broadcasted_iota(jnp.int32, (BLK, BLK), 0) <= lax.broadcasted_iota(
        jnp.int32, (BLK, BLK), 1
    )
    blank = jnp.zeros((BLK, HEAD_DIM), jnp.bfloat16)

    def place_of(block):
        run = lax.div(block, stretch)
        local = block - run * stretch
        owner = run
        if late:
            is_late = run >= shards
            owner = jnp.where(is_late, 2 * shards - 1 - run, run)
            local = local + jnp.where(is_late, stretch, 0)
        apart = owner ^ device
        slot = lax.rem(apart, members) * groups + lax.div(apart, members)
        return pl.multiple_of(slot * rows + local * BLK, BLK)

    def step(s, _):
        asker = device ^ (s * members)
        first = (2 * shards - 1 - asker if late else asker) * stretch
        units = range(stretch)
        listed = []
        for n in units:
            block = first + n
            listed.append([block, block - 1] + [links[block, i] for i in range(LINKS)])
        places = [[place_of(jnp.maximum(j, 0)) for j in row] for row in listed]
        pairs = [jnp.concatenate([pair_buf[pl.ds(p, BLK), :] for p in row], 0) for row in places]
        wide = []
        for n in units:
            ask = ask_buf[pl.ds(pl.multiple_of(s * half + n * BLK, BLK), BLK), :]
            wide.append(
                jnp.concatenate(
                    [
                        jnp.concatenate([ask[:, :HEAD_DIM], blank], 1),
                        jnp.concatenate([blank, ask[:, HEAD_DIM:]], 1),
                    ],
                    0,
                )
            )
        both = [dot(pairs[n], wide[n], ((1,), (1,))) for n in units]
        dscore_b, terms = [], []
        for n in units:
            raw = [both[n][i * BLK : (i + 1) * BLK, :BLK] for i in range(SPAN)]
            dprob = both[n][:, BLK:].reshape(SPAN, BLK, BLK)
            raw[0] = jnp.where(causal, raw[0], NEG_FILL)
            unused = [0.0] + [jnp.where(j >= 0, 0.0, NEG_FILL) for j in listed[n][1:]]
            tops = [jnp.max(raw[i], axis=0, keepdims=True) + unused[i] for i in range(SPAN)]
            top = functools.reduce(jnp.maximum, tops)
            weight = jnp.stack(
                [
                    jnp.exp2((raw[i] - (top - unused[i])) * (scaling * math.log2(math.e)))
                    for i in range(SPAN)
                ]
            )
            share = 1.0 / jnp.sum(weight, axis=(0, 1), keepdims=True)
            delta = jnp.sum(weight * dprob, axis=(0, 1), keepdims=True) * share
            prob = weight * share
            dscore = (prob * (dprob - delta)).astype(jnp.bfloat16).reshape(SPAN * BLK, BLK)
            dscore_b.append(dscore)
            prob = prob.astype(jnp.bfloat16).reshape(SPAN * BLK, BLK)
            terms.append(dot(jnp.concatenate([dscore, prob], 1), wide[n], ((1,), (0,))))
        dq = [dot(dscore_b[n], pairs[n][:, :HEAD_DIM], ((0,), (0,))) * scaling for n in units]
        for n in units:
            lanes = slice(n % 2 * HEAD_DIM, (n % 2 + 1) * HEAD_DIM)
            packed = pl.ds(pl.multiple_of(s * (half // 2) + n // 2 * BLK, BLK), BLK)
            dq_buf[packed, lanes] = dq[n].astype(jnp.bfloat16)
            for i, p in enumerate(places[n]):
                acc[pl.ds(p, BLK), :] += terms[n][i * BLK : (i + 1) * BLK]
        return 0

    lax.fori_loop(0, groups, step, 0)

    quarter = half // 2
    for s in range(groups):
        if late:
            dq_outs[s][:quarter] = dq_early[s][...]
        dq_outs[s][-quarter:] = dq_buf[s * quarter : (s + 1) * quarter, :]
    if late:
        for s in range(groups):
            own_outs[s][...] = acc[s * rows : (s + 1) * rows, :].astype(jnp.bfloat16)
        for r in range(1, members):
            for s in range(groups):
                start = (r * groups + s) * rows
                far_outs[r - 1][s] = acc[start : start + rows, :].astype(jnp.bfloat16)


def attend(links, packs, dq_early, buffers, shards, members, groups):
    late = len(buffers) > 0
    half = packs[0].shape[0] // 2
    rows = 2 * half
    slots = members * groups
    blocks = groups * half // BLK
    near = slots * rows <= 4096

    def shape(*dims, dtype=jnp.bfloat16):
        return jax.ShapeDtypeStruct((*dims, 2 * HEAD_DIM), dtype)

    outs = [shape(half if late else half // 2)] * groups
    if late:
        outs += [shape(rows)] * groups + [shape(groups, rows)] * (members - 1)
    outs += [shape(slots * rows), shape(slots * rows, dtype=jnp.float32)]
    vmem = pl.BlockSpec(memory_space=pltpu.VMEM)
    read = vmem if near else pl.BlockSpec(memory_space=pl.ANY)
    given = [*packs, *dq_early, *buffers]
    found = pl.pallas_call(
        functools.partial(attend_kernel, late, near, shards, members, groups, half),
        out_shape=outs,
        in_specs=[pl.BlockSpec(memory_space=pltpu.SMEM)]
        + [read] * len(packs)
        + [vmem] * (len(dq_early) + len(buffers)),
        out_specs=[vmem] * len(outs),
        input_output_aliases={len(given) - 1: len(outs) - 2, len(given): len(outs) - 1}
        if late
        else {},
        scratch_shapes=[
            pltpu.VMEM((groups * half, 2 * HEAD_DIM), jnp.bfloat16),
            pltpu.VMEM((groups * half // 2, 2 * HEAD_DIM), jnp.bfloat16),
            pltpu.SemaphoreType.DMA((slots + groups,)),
        ],
        compiler_params=pltpu.CompilerParams(vmem_limit_bytes=SMALL_LIMIT),
        cost_estimate=pl.CostEstimate(
            flops=10 * blocks * SPAN * BLK * BLK * HEAD_DIM if late else 0,
            bytes_accessed=8 * slots * rows * HEAD_DIM if late else 0,
            transcendentals=blocks * SPAN * BLK * BLK if late else 0,
        ),
        name="attend_late" if late else "attend_early",
    )(links, *given)
    if late:
        return found[:groups], found[groups : 2 * groups], found[2 * groups : -2]
    return found[:groups], found[-2:]


def to_chips(parts, members):
    return [parts[0]] + [swapped(part, s * members) for s, part in enumerate(parts[1:], 1)]


def with_members(parts, members):
    return parts + [swapped(part, r) for r in range(1, members) for part in parts]


def per_device(query, key, value, out_grad, links):
    rows, width = query.shape
    groups = width // HEAD_DIM
    shards = lax.axis_size("ctx")
    members = shards // groups
    arrays = (query, key, value, out_grad)

    early = split_heads(0, arrays, [], members, groups)
    late = split_heads(1, arrays, early[:1], members, groups)
    early = with_members(to_chips(early, members), members)
    late = to_chips(late, members)
    dq_early, buffers = attend(links, early, [], [], shards, members, groups)
    lent = only_pairs(late, dq_early[:1], groups)
    late = late + [swapped(lent, r) for r in range(1, members)]
    dqs, own, far = attend(links, late, dq_early, buffers, shards, members, groups)
    far = [swapped(part, r) for r, part in enumerate(far, 1)]
    dqs = to_chips(dqs, members)
    pairs = to_chips(add_partials(far, own, members, groups), members)
    return tuple(join_heads(dqs, pairs, members, groups))


def solution(mesh):
    return jax.shard_map(
        per_device,
        mesh=mesh,
        in_specs=(P("ctx", "head"), P("ctx", "head"), P("ctx", "head"), P("ctx", "head"), P()),
        out_specs=(P("ctx", "head"), P("ctx", "head"), P("ctx", "head")),
        check_vma=False,
    )
```

```python
import functools
import math

import jax
import jax.numpy as jnp
from jax import lax
from jax.experimental import pallas as pl
from jax.experimental.pallas import tpu as pltpu
from jax.sharding import PartitionSpec as P

HEAD_DIM = 128
BLK = 128
WIN = 2
LINKS = 6
SPAN = WIN + LINKS
NEG_FILL = -1e30
LATE_PAD = 16
SPLIT_LIMIT = 56 * 1024 * 1024
SMALL_LIMIT = 16 * 1024 * 1024


def swapped(x, by):
    count = lax.axis_size("ctx")
    return lax.ppermute(x, "ctx", [(i, i ^ by) for i in range(count)])


def apart(s, groups):
    return lax.rem(groups - s, groups)


def chip_column(members, groups, s):
    chip = lax.div(lax.axis_index("ctx"), members)
    return pl.ds(pl.multiple_of((chip ^ (-s % groups)) * HEAD_DIM, HEAD_DIM), HEAD_DIM)


def all_started(moves, sems):
    copies = [
        pltpu.make_async_copy(source, target, sems.at[i])
        for i, (source, target) in enumerate(moves)
    ]
    for copy in copies:
        copy.start()
    return copies


def fill_pack(out, held, at, column):
    query, key, value, grad = held
    half = at.stop - at.start
    for t, (pair, ask) in enumerate(((key, query), (value, grad))):
        lanes = slice(t * HEAD_DIM, (t + 1) * HEAD_DIM)
        out[:half, lanes] = pair[at, column]
        out[half : 2 * half, lanes] = ask[at, column]


def split_first_kernel(members, groups, *refs):
    held, sems = refs[4 + groups - 1 : -1], refs[-1]
    half = held[0].shape[0]
    for copy in all_started(
        [(array.at[pl.ds(0, half)], buf) for array, buf in zip(refs[:4], held)], sems
    ):
        copy.wait()
    for s in range(1, groups):
        column = chip_column(members, groups, s)
        fill_pack(refs[4 + s - 1], held, slice(0, half), column)


def split_rest_kernel(members, groups, *refs):
    held = refs[:4]
    own, late = refs[4], refs[5:]
    rows = held[0].shape[0]
    half = rows // 2
    fill_pack(own, held, slice(0, half), chip_column(members, groups, 0))
    for s in range(groups):
        fill_pack(late[s], held, slice(half, rows), chip_column(members, groups, s))
        late[s][rows:, :] = jnp.zeros_like(late[s][rows:, :])


def split_heads(arrays, members, groups):
    rows, width = arrays[0].shape
    half = rows // 2
    out = jax.ShapeDtypeStruct((rows, 2 * HEAD_DIM), jnp.bfloat16)
    longer = jax.ShapeDtypeStruct((rows + LATE_PAD, 2 * HEAD_DIM), jnp.bfloat16)
    vmem = pl.BlockSpec(memory_space=pltpu.VMEM)
    early = pl.pallas_call(
        functools.partial(split_first_kernel, members, groups),
        out_shape=[out] * (groups - 1),
        in_specs=[pl.BlockSpec(memory_space=pl.ANY)] * 4,
        out_specs=[vmem] * (groups - 1),
        scratch_shapes=[pltpu.VMEM((half, width), array.dtype) for array in arrays]
        + [pltpu.SemaphoreType.DMA((4,))],
        compiler_params=pltpu.CompilerParams(vmem_limit_bytes=SPLIT_LIMIT),
        cost_estimate=pl.CostEstimate(
            flops=0, bytes_accessed=16 * half * width, transcendentals=0
        ),
        name="split_first",
    )(*arrays)
    own, *late = pl.pallas_call(
        functools.partial(split_rest_kernel, members, groups),
        out_shape=[out] + [longer] * groups,
        in_specs=[vmem] * 4,
        out_specs=[vmem] * (groups + 1),
        compiler_params=pltpu.CompilerParams(vmem_limit_bytes=SMALL_LIMIT),
        cost_estimate=pl.CostEstimate(
            flops=0, bytes_accessed=16 * half * width, transcendentals=0
        ),
        name="split_rest",
    )(*arrays)
    return [own, *early], late


def pairs_kernel(groups, *refs):
    outs = refs[-(groups // 2) :]
    for s in range(groups):
        out = outs[s // 2]
        out[s % 2] = refs[s][: out.shape[1], :]


def only_pairs(packs, half, after, groups):
    hbm = pl.BlockSpec(memory_space=pl.ANY)
    vmem = pl.BlockSpec(memory_space=pltpu.VMEM)
    outs = groups // 2
    return pl.pallas_call(
        functools.partial(pairs_kernel, groups),
        out_shape=[jax.ShapeDtypeStruct((2, half, 2 * HEAD_DIM), jnp.bfloat16)] * outs,
        in_specs=[vmem] * groups + [hbm] * len(after),
        out_specs=[vmem] * outs,
        compiler_params=pltpu.CompilerParams(vmem_limit_bytes=SMALL_LIMIT),
        cost_estimate=pl.CostEstimate(
            flops=0, bytes_accessed=8 * groups * half * HEAD_DIM, transcendentals=0
        ),
        name="only_pairs",
    )(*packs, *after)


def join_queries_kernel(members, groups, *refs):
    out, token = refs[-2:]
    token[...] = jnp.zeros_like(token)
    for s in range(groups):
        column = chip_column(members, groups, s)
        for n in range(out.shape[0] // BLK):
            packed = slice(n // 2 * BLK, (n // 2 + 1) * BLK)
            lanes = slice(n % 2 * HEAD_DIM, (n % 2 + 1) * HEAD_DIM)
            out[n * BLK : (n + 1) * BLK, column] = refs[s][packed, lanes]


def join_pairs_kernel(members, groups, *refs):
    outs = refs[-2:]
    for s in range(groups):
        column = chip_column(members, groups, s)
        outs[0][:, column] = refs[s][:, :HEAD_DIM]
        outs[1][:, column] = refs[s][:, HEAD_DIM:]


def join_heads(dqs, pairs, members, groups):
    rows = pairs[0].shape[0]
    vmem = pl.BlockSpec(memory_space=pltpu.VMEM)
    out = jax.ShapeDtypeStruct((rows, groups * HEAD_DIM), jnp.bfloat16)
    token = jax.ShapeDtypeStruct((8, HEAD_DIM), jnp.float32)
    bytes_out = 2 * rows * groups * HEAD_DIM
    query_grad, token = pl.pallas_call(
        functools.partial(join_queries_kernel, members, groups),
        out_shape=[out, token],
        in_specs=[vmem] * groups,
        out_specs=[vmem] * 2,
        compiler_params=pltpu.CompilerParams(vmem_limit_bytes=SMALL_LIMIT),
        cost_estimate=pl.CostEstimate(
            flops=0, bytes_accessed=200 * bytes_out, transcendentals=0
        ),
        name="join_queries",
    )(*dqs)
    key_grad, value_grad = pl.pallas_call(
        functools.partial(join_pairs_kernel, members, groups),
        out_shape=[out] * 2,
        in_specs=[vmem] * (groups + 1),
        out_specs=[vmem] * 2,
        compiler_params=pltpu.CompilerParams(vmem_limit_bytes=SMALL_LIMIT),
        cost_estimate=pl.CostEstimate(flops=0, bytes_accessed=4 * bytes_out, transcendentals=0),
        name="join_pairs",
    )(*pairs, token)
    return query_grad, key_grad, value_grad


def add_kernel(members, groups, *refs):
    far = refs[: members - 1]
    own = refs[members - 1 : members - 1 + groups]
    outs = refs[members - 1 + groups :]
    for s in range(groups):
        total = own[s][...].astype(jnp.float32)
        for part in far:
            total = total + part[s].astype(jnp.float32)
        outs[s][:, :HEAD_DIM] = (total[:, :HEAD_DIM] * HEAD_DIM**-0.5).astype(jnp.bfloat16)
        outs[s][:, HEAD_DIM:] = total[:, HEAD_DIM:].astype(jnp.bfloat16)


def add_partials(far, own, members, groups):
    vmem = pl.BlockSpec(memory_space=pltpu.VMEM)
    out = jax.ShapeDtypeStruct(own[0].shape, jnp.bfloat16)
    return pl.pallas_call(
        functools.partial(add_kernel, members, groups),
        out_shape=[out] * groups,
        in_specs=[vmem] * (members - 1 + groups),
        out_specs=[vmem] * groups,
        compiler_params=pltpu.CompilerParams(vmem_limit_bytes=SMALL_LIMIT),
        cost_estimate=pl.CostEstimate(
            flops=0, bytes_accessed=8 * groups * own[0].size, transcendentals=0
        ),
        name="add_partials",
    )(*far, *own)


def dot(left, right, dims):
    return lax.dot_general(left, right, (dims, ((), ())), preferred_element_type=jnp.float32)


def attend_kernel(late, near, shards, members, groups, half, *refs):
    slots = members * groups
    rows = 2 * half
    stretch = half // BLK
    links = refs[0]
    packs = [*refs[1 : 1 + groups]]
    lent = (members - 1) * (groups // 2)
    for part in refs[1 + groups : 1 + groups + lent]:
        packs += [part.at[n] for n in range(2)]
    refs = refs[1 + groups + lent :]
    if late:
        dq_early = refs[:groups]
        refs = refs[groups + 2 :]
        dq_outs = refs[:groups]
        own_outs = refs[groups : 2 * groups]
        far_outs = refs[2 * groups : 2 * groups + members - 1]
        refs = refs[2 * groups + members - 1 :]
    else:
        dq_outs = refs[:groups]
        refs = refs[groups:]
    pair_buf, acc, ask_buf, dq_buf, sems = refs
    device = lax.axis_index("ctx")

    moves = []
    for s in range(groups):
        moves.append((packs[s].at[pl.ds(half, half)], ask_buf.at[pl.ds(s * half, half)]))
        for r in range(members):
            i = r * groups + s
            place = pl.ds(i * rows + (half if late else 0), half)
            moves.append((packs[i].at[pl.ds(0, half)], pair_buf.at[place]))
    by_copy = 0 if near else len(moves)
    copies = all_started(moves[:by_copy], sems)
    for source, target in moves[by_copy:]:
        target[...] = source[...]
    if not late:
        acc[...] = jnp.zeros_like(acc)
    for copy in copies:
        copy.wait()

    scaling = HEAD_DIM**-0.5
    causal = lax.broadcasted_iota(jnp.int32, (BLK, BLK), 0) <= lax.broadcasted_iota(
        jnp.int32, (BLK, BLK), 1
    )
    blank = jnp.zeros((BLK, HEAD_DIM), jnp.bfloat16)

    def place_of(block):
        run = lax.div(block, stretch)
        local = block - run * stretch
        owner = run
        if late:
            is_late = run >= shards
            owner = jnp.where(is_late, 2 * shards - 1 - run, run)
            local = local + jnp.where(is_late, stretch, 0)
        bits = owner ^ device
        slot = lax.rem(bits, members) * groups + apart(lax.div(bits, members), groups)
        return pl.multiple_of(slot * rows + local * BLK, BLK)

    def step(s, _):
        asker = device ^ (apart(s, groups) * members)
        first = (2 * shards - 1 - asker if late else asker) * stretch
        units = range(stretch)
        listed = []
        for n in units:
            block = first + n
            listed.append([block, block - 1] + [links[block, i] for i in range(LINKS)])
        places = [[place_of(jnp.maximum(j, 0)) for j in row] for row in listed]
        pairs = [jnp.concatenate([pair_buf[pl.ds(p, BLK), :] for p in row], 0) for row in places]
        wide = []
        for n in units:
            ask = ask_buf[pl.ds(pl.multiple_of(s * half + n * BLK, BLK), BLK), :]
            wide.append(
                jnp.concatenate(
                    [
                        jnp.concatenate([ask[:, :HEAD_DIM], blank], 1),
                        jnp.concatenate([blank, ask[:, HEAD_DIM:]], 1),
                    ],
                    0,
                )
            )
        both = [dot(pairs[n], wide[n], ((1,), (1,))) for n in units]
        dscore_b, terms = [], []
        for n in units:
            raw = [both[n][i * BLK : (i + 1) * BLK, :BLK] for i in range(SPAN)]
            dprob = both[n][:, BLK:].reshape(SPAN, BLK, BLK)
            raw[0] = jnp.where(causal, raw[0], NEG_FILL)
            unused = [0.0] + [jnp.where(j >= 0, 0.0, NEG_FILL) for j in listed[n][1:]]
            tops = [jnp.max(raw[i], axis=0, keepdims=True) + unused[i] for i in range(SPAN)]
            top = functools.reduce(jnp.maximum, tops)
            weight = jnp.stack(
                [
                    jnp.exp2((raw[i] - (top - unused[i])) * (scaling * math.log2(math.e)))
                    for i in range(SPAN)
                ]
            )
            share = 1.0 / jnp.sum(weight, axis=(0, 1), keepdims=True)
            delta = jnp.sum(weight * dprob, axis=(0, 1), keepdims=True) * share
            prob = weight * share
            dscore = (prob * (dprob - delta)).astype(jnp.bfloat16).reshape(SPAN * BLK, BLK)
            dscore_b.append(dscore)
            prob = prob.astype(jnp.bfloat16).reshape(SPAN * BLK, BLK)
            terms.append(dot(jnp.concatenate([dscore, prob], 1), wide[n], ((1,), (0,))))
        dq = [dot(dscore_b[n], pairs[n][:, :HEAD_DIM], ((0,), (0,))) * scaling for n in units]
        for n in units:
            lanes = slice(n % 2 * HEAD_DIM, (n % 2 + 1) * HEAD_DIM)
            packed = pl.ds(pl.multiple_of(s * (half // 2) + n // 2 * BLK, BLK), BLK)
            dq_buf[packed, lanes] = dq[n].astype(jnp.bfloat16)
            for i, p in enumerate(places[n]):
                acc[pl.ds(p, BLK), :] += terms[n][i * BLK : (i + 1) * BLK]
        return 0

    lax.fori_loop(0, groups, step, 0)

    quarter = half // 2
    for s in range(groups):
        if late:
            dq_outs[s][:quarter] = dq_early[s][...]
        dq_outs[s][-quarter:] = dq_buf[s * quarter : (s + 1) * quarter, :]
    if late:
        for s in range(groups):
            own_outs[s][...] = acc[s * rows : (s + 1) * rows, :].astype(jnp.bfloat16)
        for r in range(1, members):
            for s in range(groups):
                start = (r * groups + s) * rows
                far_outs[r - 1][s] = acc[start : start + rows, :].astype(jnp.bfloat16)


def attend(links, packs, dq_early, buffers, rows, shards, members, groups):
    late = len(buffers) > 0
    half = rows // 2
    slots = members * groups
    blocks = groups * half // BLK
    near = slots * rows <= 4096

    def shape(*dims, dtype=jnp.bfloat16):
        return jax.ShapeDtypeStruct((*dims, 2 * HEAD_DIM), dtype)

    outs = [shape(half if late else half // 2)] * groups
    if late:
        outs += [shape(rows)] * groups + [shape(groups, rows)] * (members - 1)
    outs += [shape(slots * rows), shape(slots * rows, dtype=jnp.float32)]
    vmem = pl.BlockSpec(memory_space=pltpu.VMEM)
    read = vmem if near else pl.BlockSpec(memory_space=pl.ANY)
    given = [*packs, *dq_early, *buffers]
    found = pl.pallas_call(
        functools.partial(attend_kernel, late, near, shards, members, groups, half),
        out_shape=outs,
        in_specs=[pl.BlockSpec(memory_space=pltpu.SMEM)]
        + [read] * len(packs)
        + [vmem] * (len(dq_early) + len(buffers)),
        out_specs=[vmem] * len(outs),
        input_output_aliases={len(given) - 1: len(outs) - 2, len(given): len(outs) - 1}
        if late
        else {},
        scratch_shapes=[
            pltpu.VMEM((groups * half, 2 * HEAD_DIM), jnp.bfloat16),
            pltpu.VMEM((groups * half // 2, 2 * HEAD_DIM), jnp.bfloat16),
            pltpu.SemaphoreType.DMA((slots + groups,)),
        ],
        compiler_params=pltpu.CompilerParams(vmem_limit_bytes=SMALL_LIMIT),
        cost_estimate=pl.CostEstimate(
            flops=10 * blocks * SPAN * BLK * BLK * HEAD_DIM if late else 0,
            bytes_accessed=8 * slots * rows * HEAD_DIM if late else 0,
            transcendentals=blocks * SPAN * BLK * BLK if late else 0,
        ),
        name="attend_late" if late else "attend_early",
    )(links, *given)
    if late:
        return found[:groups], found[groups : 2 * groups], found[2 * groups : -2]
    return found[:groups], found[-2:]


def to_chips(parts, members):
    groups = len(parts)
    return [swapped(part, -s % groups * members) if s else part for s, part in enumerate(parts)]


def with_members(parts, members):
    return [swapped(part, r) for r in range(1, members) for part in parts]


def per_device(query, key, value, out_grad, links):
    rows, width = query.shape
    groups = width // HEAD_DIM
    shards = lax.axis_size("ctx")
    members = shards // groups
    arrays = (query, key, value, out_grad)

    early, late = split_heads(arrays, members, groups)
    early = to_chips(early, members)
    late = to_chips(late, members)
    early = early + with_members(only_pairs(early, rows // 2, [], groups), members)
    dq_early, buffers = attend(links, early, [], [], rows, shards, members, groups)
    late = late + with_members(only_pairs(late, rows // 2, dq_early[:1], groups), members)
    dqs, own, far = attend(links, late, dq_early, buffers, rows, shards, members, groups)
    far = [swapped(part, r) for r, part in enumerate(far, 1)]
    dqs = to_chips(dqs, members)
    pairs = to_chips(add_partials(far, own, members, groups), members)
    return join_heads(dqs, pairs, members, groups)


def solution(mesh):
    return jax.shard_map(
        per_device,
        mesh=mesh,
        in_specs=(P("ctx", "head"), P("ctx", "head"), P("ctx", "head"), P("ctx", "head"), P()),
        out_specs=(P("ctx", "head"), P("ctx", "head"), P("ctx", "head")),
        check_vma=False,
    )
```

```python
import functools

import jax
import jax.numpy as jnp
from jax import lax
from jax.experimental import pallas as pl
from jax.experimental.pallas import tpu as pltpu
from jax.sharding import PartitionSpec as P

HEAD_DIM = 128
BLK = 128
WIN = 2
LINKS = 6
SPAN = WIN + LINKS
NEG_FILL = -1e30
LATE_PAD = 16
SPLIT_LIMIT = 56 * 1024 * 1024
SMALL_LIMIT = 16 * 1024 * 1024


def swapped(x, by):
    count = lax.axis_size("ctx")
    return lax.ppermute(x, "ctx", [(i, i ^ by) for i in range(count)])


def apart(s, groups):
    return lax.rem(groups - s, groups)


def chip_column(members, groups, s):
    chip = lax.div(lax.axis_index("ctx"), members)
    return pl.ds(pl.multiple_of((chip ^ (-s % groups)) * HEAD_DIM, HEAD_DIM), HEAD_DIM)


def all_started(moves, sems):
    copies = [
        pltpu.make_async_copy(source, target, sems.at[i])
        for i, (source, target) in enumerate(moves)
    ]
    for copy in copies:
        copy.start()
    return copies


def fill_pack(out, held, at, column):
    query, key, value, grad = held
    half = at.stop - at.start
    for t, (pair, ask) in enumerate(((key, query), (value, grad))):
        lanes = slice(t * HEAD_DIM, (t + 1) * HEAD_DIM)
        out[:half, lanes] = pair[at, column]
        out[half : 2 * half, lanes] = ask[at, column]


def split_first_kernel(members, groups, *refs):
    held, sems = refs[4 + groups - 1 : -1], refs[-1]
    half = held[0].shape[0]
    for copy in all_started(
        [(array.at[pl.ds(0, half)], buf) for array, buf in zip(refs[:4], held)], sems
    ):
        copy.wait()
    for s in range(1, groups):
        column = chip_column(members, groups, s)
        fill_pack(refs[4 + s - 1], held, slice(0, half), column)


def split_rest_kernel(members, groups, *refs):
    held = refs[:4]
    own, late = refs[4], refs[5:]
    rows = held[0].shape[0]
    half = rows // 2
    fill_pack(own, held, slice(0, half), chip_column(members, groups, 0))
    for s in range(groups):
        fill_pack(late[s], held, slice(half, rows), chip_column(members, groups, s))
        late[s][rows:, :] = jnp.zeros_like(late[s][rows:, :])


def split_heads(arrays, members, groups):
    rows, width = arrays[0].shape
    half = rows // 2
    out = jax.ShapeDtypeStruct((rows, 2 * HEAD_DIM), jnp.bfloat16)
    longer = jax.ShapeDtypeStruct((rows + LATE_PAD, 2 * HEAD_DIM), jnp.bfloat16)
    vmem = pl.BlockSpec(memory_space=pltpu.VMEM)
    early = pl.pallas_call(
        functools.partial(split_first_kernel, members, groups),
        out_shape=[out] * (groups - 1),
        in_specs=[pl.BlockSpec(memory_space=pl.ANY)] * 4,
        out_specs=[vmem] * (groups - 1),
        scratch_shapes=[pltpu.VMEM((half, width), array.dtype) for array in arrays]
        + [pltpu.SemaphoreType.DMA((4,))],
        compiler_params=pltpu.CompilerParams(vmem_limit_bytes=SPLIT_LIMIT),
        cost_estimate=pl.CostEstimate(
            flops=0, bytes_accessed=16 * half * width, transcendentals=0
        ),
        name="split_first",
    )(*arrays)
    own, *late = pl.pallas_call(
        functools.partial(split_rest_kernel, members, groups),
        out_shape=[out] + [longer] * groups,
        in_specs=[vmem] * 4,
        out_specs=[vmem] * (groups + 1),
        compiler_params=pltpu.CompilerParams(vmem_limit_bytes=SMALL_LIMIT),
        cost_estimate=pl.CostEstimate(
            flops=0, bytes_accessed=16 * half * width, transcendentals=0
        ),
        name="split_rest",
    )(*arrays)
    return [own, *early], late


def pairs_kernel(groups, *refs):
    outs = refs[-(groups // 2) :]
    for s in range(groups):
        out = outs[s // 2]
        out[s % 2] = refs[s][: out.shape[1], :]


def only_pairs(packs, half, after, groups):
    hbm = pl.BlockSpec(memory_space=pl.ANY)
    vmem = pl.BlockSpec(memory_space=pltpu.VMEM)
    outs = groups // 2
    return pl.pallas_call(
        functools.partial(pairs_kernel, groups),
        out_shape=[jax.ShapeDtypeStruct((2, half, 2 * HEAD_DIM), jnp.bfloat16)] * outs,
        in_specs=[vmem] * groups + [hbm] * len(after),
        out_specs=[vmem] * outs,
        compiler_params=pltpu.CompilerParams(vmem_limit_bytes=SMALL_LIMIT),
        cost_estimate=pl.CostEstimate(
            flops=0, bytes_accessed=8 * groups * half * HEAD_DIM, transcendentals=0
        ),
        name="only_pairs",
    )(*packs, *after)


def join_queries_kernel(members, groups, *refs):
    out, token = refs[-2:]
    token[...] = jnp.zeros_like(token)
    for s in range(groups):
        column = chip_column(members, groups, s)
        for n in range(out.shape[0] // BLK):
            packed = slice(n // 2 * BLK, (n // 2 + 1) * BLK)
            lanes = slice(n % 2 * HEAD_DIM, (n % 2 + 1) * HEAD_DIM)
            out[n * BLK : (n + 1) * BLK, column] = refs[s][packed, lanes]


def join_pairs_kernel(members, groups, *refs):
    outs = refs[-2:]
    half = refs[0].shape[0]
    for h in range(2):
        at = slice(h * half, (h + 1) * half)
        for s in range(groups):
            column = chip_column(members, groups, s)
            outs[0][at, column] = refs[h * groups + s][:, :HEAD_DIM]
            outs[1][at, column] = refs[h * groups + s][:, HEAD_DIM:]


def join_heads(dqs, pairs, members, groups):
    rows = 2 * pairs[0].shape[0]
    vmem = pl.BlockSpec(memory_space=pltpu.VMEM)
    out = jax.ShapeDtypeStruct((rows, groups * HEAD_DIM), jnp.bfloat16)
    token = jax.ShapeDtypeStruct((8, HEAD_DIM), jnp.float32)
    bytes_out = 2 * rows * groups * HEAD_DIM
    query_grad, token = pl.pallas_call(
        functools.partial(join_queries_kernel, members, groups),
        out_shape=[out, token],
        in_specs=[vmem] * groups,
        out_specs=[vmem] * 2,
        compiler_params=pltpu.CompilerParams(vmem_limit_bytes=SMALL_LIMIT),
        cost_estimate=pl.CostEstimate(
            flops=0, bytes_accessed=200 * bytes_out, transcendentals=0
        ),
        name="join_queries",
    )(*dqs)
    key_grad, value_grad = pl.pallas_call(
        functools.partial(join_pairs_kernel, members, groups),
        out_shape=[out] * 2,
        in_specs=[vmem] * (2 * groups + 1),
        out_specs=[vmem] * 2,
        compiler_params=pltpu.CompilerParams(vmem_limit_bytes=SMALL_LIMIT),
        cost_estimate=pl.CostEstimate(flops=0, bytes_accessed=4 * bytes_out, transcendentals=0),
        name="join_pairs",
    )(*pairs, token)
    return query_grad, key_grad, value_grad


def add_kernel(members, groups, *refs):
    far = refs[: members - 1]
    own = refs[members - 1 : members - 1 + groups]
    outs = refs[members - 1 + groups :]
    half = outs[0].shape[0]
    for h in range(2):
        at = slice(h * half, (h + 1) * half)
        for s in range(groups):
            total = own[s][at, :].astype(jnp.float32)
            for part in far:
                total = total + part[s, at, :].astype(jnp.float32)
            out = outs[h * groups + s]
            out[:, :HEAD_DIM] = (total[:, :HEAD_DIM] * HEAD_DIM**-0.5).astype(jnp.bfloat16)
            out[:, HEAD_DIM:] = total[:, HEAD_DIM:].astype(jnp.bfloat16)


def add_partials(far, own, members, groups):
    vmem = pl.BlockSpec(memory_space=pltpu.VMEM)
    rows = own[0].shape[0]
    out = jax.ShapeDtypeStruct((rows // 2, 2 * HEAD_DIM), jnp.bfloat16)
    found = pl.pallas_call(
        functools.partial(add_kernel, members, groups),
        out_shape=[out] * (2 * groups),
        in_specs=[vmem] * (members - 1 + groups),
        out_specs=[vmem] * (2 * groups),
        compiler_params=pltpu.CompilerParams(vmem_limit_bytes=SMALL_LIMIT),
        cost_estimate=pl.CostEstimate(
            flops=0, bytes_accessed=8 * groups * own[0].size, transcendentals=0
        ),
        name="add_partials",
    )(*far, *own)
    return found[:groups], found[groups:]


def dot(left, right, dims):
    return lax.dot_general(left, right, (dims, ((), ())), preferred_element_type=jnp.float32)


def attend_kernel(late, near, shards, members, groups, half, *refs):
    slots = members * groups
    rows = 2 * half
    stretch = half // BLK
    links = refs[0]
    packs = [*refs[1 : 1 + groups]]
    lent = (members - 1) * (groups // 2)
    for part in refs[1 + groups : 1 + groups + lent]:
        packs += [part.at[n] for n in range(2)]
    refs = refs[1 + groups + lent :]
    if late:
        dq_early = refs[:groups]
        refs = refs[groups + 2 :]
        dq_outs = refs[:groups]
        own_outs = refs[groups : 2 * groups]
        far_outs = refs[2 * groups : 2 * groups + members - 1]
        refs = refs[2 * groups + members - 1 :]
    else:
        dq_outs = refs[:groups]
        refs = refs[groups:]
    pair_buf, acc, ask_buf, dq_buf, sems = refs
    device = lax.axis_index("ctx")

    moves = []
    for s in range(groups):
        moves.append((packs[s].at[pl.ds(half, half)], ask_buf.at[pl.ds(s * half, half)]))
        for r in range(members):
            i = r * groups + s
            place = pl.ds(i * rows + (half if late else 0), half)
            moves.append((packs[i].at[pl.ds(0, half)], pair_buf.at[place]))
    by_copy = 0 if near else len(moves)
    copies = all_started(moves[:by_copy], sems)
    for source, target in moves[by_copy:]:
        target[...] = source[...]
    if not late:
        acc[...] = jnp.zeros_like(acc)
    for copy in copies:
        copy.wait()

    scaling = HEAD_DIM**-0.5
    causal = lax.broadcasted_iota(jnp.int32, (BLK, BLK), 0) <= lax.broadcasted_iota(
        jnp.int32, (BLK, BLK), 1
    )

    def place_of(block):
        run = lax.div(block, stretch)
        local = block - run * stretch
        owner = run
        if late:
            is_late = run >= shards
            owner = jnp.where(is_late, 2 * shards - 1 - run, run)
            local = local + jnp.where(is_late, stretch, 0)
        bits = owner ^ device
        slot = lax.rem(bits, members) * groups + apart(lax.div(bits, members), groups)
        return pl.multiple_of(slot * rows + local * BLK, BLK)

    def step(s, _):
        asker = device ^ (apart(s, groups) * members)
        first = (2 * shards - 1 - asker if late else asker) * stretch
        units = range(stretch)
        listed = []
        for n in units:
            block = first + n
            listed.append([block, block - 1] + [links[block, i] for i in range(LINKS)])
        places = [[place_of(jnp.maximum(j, 0)) for j in row] for row in listed]
        pairs = [jnp.concatenate([pair_buf[pl.ds(p, BLK), :] for p in row], 0) for row in places]
        asks = [
            ask_buf[pl.ds(pl.multiple_of(s * half + n * BLK, BLK), BLK), :] for n in units
        ]
        raws = [dot(pairs[n][:, :HEAD_DIM], asks[n][:, :HEAD_DIM], ((1,), (1,))) for n in units]
        dprobs = [dot(pairs[n][:, HEAD_DIM:], asks[n][:, HEAD_DIM:], ((1,), (1,))) for n in units]
        dscore_b, terms = [], []
        for n in units:
            raw = [raws[n][i * BLK : (i + 1) * BLK] for i in range(SPAN)]
            dprob = dprobs[n].reshape(SPAN, BLK, BLK)
            raw[0] = jnp.where(causal, raw[0], NEG_FILL)
            unused = [0.0] + [jnp.where(j >= 0, 0.0, NEG_FILL) for j in listed[n][1:]]
            tops = [jnp.max(raw[i], axis=0, keepdims=True) + unused[i] for i in range(SPAN)]
            top = functools.reduce(jnp.maximum, tops)
            weight = jnp.stack(
                [
                    jnp.exp((raw[i] - (top - unused[i])) * scaling)
                    for i in range(SPAN)
                ]
            )
            share = 1.0 / jnp.sum(weight, axis=(0, 1), keepdims=True)
            delta = jnp.sum(weight * dprob, axis=(0, 1), keepdims=True) * share
            prob = weight * share
            dscore = (prob * (dprob - delta)).astype(jnp.bfloat16).reshape(SPAN * BLK, BLK)
            dscore_b.append(dscore)
            prob = prob.astype(jnp.bfloat16).reshape(SPAN * BLK, BLK)
            dk = dot(dscore, asks[n][:, :HEAD_DIM], ((1,), (0,)))
            dv = dot(prob, asks[n][:, HEAD_DIM:], ((1,), (0,)))
            terms.append(jnp.concatenate([dk, dv], 1))
        dq = [dot(dscore_b[n], pairs[n][:, :HEAD_DIM], ((0,), (0,))) * scaling for n in units]
        for n in units:
            lanes = slice(n % 2 * HEAD_DIM, (n % 2 + 1) * HEAD_DIM)
            packed = pl.ds(pl.multiple_of(s * (half // 2) + n // 2 * BLK, BLK), BLK)
            dq_buf[packed, lanes] = dq[n].astype(jnp.bfloat16)
            for i, p in enumerate(places[n]):
                acc[pl.ds(p, BLK), :] += terms[n][i * BLK : (i + 1) * BLK]
        return 0

    lax.fori_loop(0, groups, step, 0, unroll=2)

    quarter = half // 2
    for s in range(groups):
        if late:
            dq_outs[s][:quarter] = dq_early[s][...]
        start = quarter if late else 0
        dq_outs[s][start : start + quarter] = dq_buf[s * quarter : (s + 1) * quarter, :]
        if late:
            dq_outs[s][half:] = jnp.zeros_like(dq_outs[s][half:])
    if late:
        for s in range(groups):
            own_outs[s][...] = acc[s * rows : (s + 1) * rows, :].astype(jnp.bfloat16)
        for r in range(1, members):
            for s in range(groups):
                start = (r * groups + s) * rows
                far_outs[r - 1][s] = acc[start : start + rows, :].astype(jnp.bfloat16)


def attend(links, packs, dq_early, buffers, rows, shards, members, groups):
    late = len(buffers) > 0
    half = rows // 2
    slots = members * groups
    blocks = groups * half // BLK
    near = slots * rows <= 4096

    def shape(*dims, dtype=jnp.bfloat16):
        return jax.ShapeDtypeStruct((*dims, 2 * HEAD_DIM), dtype)

    outs = [shape(half + LATE_PAD if late else half // 2)] * groups
    if late:
        outs += [shape(rows)] * groups + [shape(groups, rows)] * (members - 1)
    outs += [shape(slots * rows), shape(slots * rows, dtype=jnp.float32)]
    vmem = pl.BlockSpec(memory_space=pltpu.VMEM)
    read = vmem if near else pl.BlockSpec(memory_space=pl.ANY)
    given = [*packs, *dq_early, *buffers]
    found = pl.pallas_call(
        functools.partial(attend_kernel, late, near, shards, members, groups, half),
        out_shape=outs,
        in_specs=[pl.BlockSpec(memory_space=pltpu.SMEM)]
        + [read] * len(packs)
        + [vmem] * (len(dq_early) + len(buffers)),
        out_specs=[vmem] * len(outs),
        input_output_aliases={len(given) - 1: len(outs) - 2, len(given): len(outs) - 1}
        if late
        else {},
        scratch_shapes=[
            pltpu.VMEM((groups * half, 2 * HEAD_DIM), jnp.bfloat16),
            pltpu.VMEM((groups * half // 2, 2 * HEAD_DIM), jnp.bfloat16),
            pltpu.SemaphoreType.DMA((slots + groups,)),
        ],
        compiler_params=pltpu.CompilerParams(vmem_limit_bytes=SMALL_LIMIT),
        cost_estimate=pl.CostEstimate(
            flops=10 * blocks * SPAN * BLK * BLK * HEAD_DIM if late else 0,
            bytes_accessed=8 * slots * rows * HEAD_DIM if late else 0,
            transcendentals=blocks * SPAN * BLK * BLK if late else 0,
        ),
        name="attend_late" if late else "attend_early",
    )(links, *given)
    if late:
        return found[:groups], found[groups : 2 * groups], found[2 * groups : -2]
    return found[:groups], found[-2:]


def to_chips(parts, members):
    groups = len(parts)
    return [swapped(part, -s % groups * members) if s else part for s, part in enumerate(parts)]


def with_members(parts, members):
    return [swapped(part, r) for r in range(1, members) for part in parts]


def per_device(query, key, value, out_grad, links):
    rows, width = query.shape
    groups = width // HEAD_DIM
    shards = lax.axis_size("ctx")
    members = shards // groups
    arrays = (query, key, value, out_grad)

    early, late = split_heads(arrays, members, groups)
    early = to_chips(early, members)
    late = to_chips(late, members)
    early = early + with_members(only_pairs(early, rows // 2, [], groups), members)
    dq_early, buffers = attend(links, early, [], [], rows, shards, members, groups)
    late = late + with_members(only_pairs(late, rows // 2, dq_early[:1], groups), members)
    dqs, own, far = attend(links, late, dq_early, buffers, rows, shards, members, groups)
    far = [swapped(part, r) for r, part in enumerate(far, 1)]
    dqs = to_chips(dqs, members)
    pairs = add_partials(far, own, members, groups)
    pairs = to_chips(pairs[0], members) + to_chips(pairs[1], members)
    return join_heads(dqs, pairs, members, groups)


def solution(mesh):
    return jax.shard_map(
        per_device,
        mesh=mesh,
        in_specs=(P("ctx", "head"), P("ctx", "head"), P("ctx", "head"), P("ctx", "head"), P()),
        out_specs=(P("ctx", "head"), P("ctx", "head"), P("ctx", "head")),
        check_vma=False,
    )
```

```python
import functools

import jax
import jax.numpy as jnp
from jax import lax
from jax.experimental import pallas as pl
from jax.experimental.pallas import tpu as pltpu
from jax.sharding import PartitionSpec as P

HEAD_DIM = 128
BLK = 128
WIN = 2
LINKS = 6
SPAN = WIN + LINKS
NEG_FILL = -1e30
LATE_PAD = 16
SPLIT_LIMIT = 56 * 1024 * 1024
SMALL_LIMIT = 16 * 1024 * 1024


def swapped(x, by):
    count = lax.axis_size("ctx")
    return lax.ppermute(x, "ctx", [(i, i ^ by) for i in range(count)])


def apart(s, groups):
    return lax.rem(groups - s, groups)


def chip_column(members, groups, s):
    chip = lax.div(lax.axis_index("ctx"), members)
    return pl.ds(pl.multiple_of((chip ^ (-s % groups)) * HEAD_DIM, HEAD_DIM), HEAD_DIM)


def all_started(moves, sems):
    copies = [
        pltpu.make_async_copy(source, target, sems.at[i])
        for i, (source, target) in enumerate(moves)
    ]
    for copy in copies:
        copy.start()
    return copies


def fill_pack(out, held, at, column):
    query, key, value, grad = held
    half = at.stop - at.start
    for t, (pair, ask) in enumerate(((key, query), (value, grad))):
        lanes = slice(t * HEAD_DIM, (t + 1) * HEAD_DIM)
        out[:half, lanes] = pair[at, column]
        out[half : 2 * half, lanes] = ask[at, column]


def split_early_kernel(members, groups, wanted, *refs):
    outs = refs[-1 - len(wanted) : -1]
    half = outs[0].shape[0] // 2
    rows = pl.ds(0, half)
    query, key, value, grad = refs[:4]
    moves = []
    for s, out in zip(wanted, outs):
        column = chip_column(members, groups, s)
        for t, (pair, ask) in enumerate(((key, query), (value, grad))):
            lanes = pl.ds(t * HEAD_DIM, HEAD_DIM)
            moves.append((pair.at[rows, column], out.at[rows, lanes]))
            moves.append((ask.at[rows, column], out.at[pl.ds(half, half), lanes]))
    for copy in all_started(moves, refs[-1]):
        copy.wait()


def split_early(wanted, arrays, after, members, groups):
    rows = arrays[0].shape[0]
    out = jax.ShapeDtypeStruct((rows, 2 * HEAD_DIM), jnp.bfloat16)
    return pl.pallas_call(
        functools.partial(split_early_kernel, members, groups, wanted),
        out_shape=[out] * len(wanted),
        in_specs=[pl.BlockSpec(memory_space=pl.ANY)] * (len(arrays) + len(after)),
        out_specs=[pl.BlockSpec(memory_space=pltpu.VMEM)] * len(wanted),
        scratch_shapes=[pltpu.SemaphoreType.DMA((4 * len(wanted),))],
        compiler_params=pltpu.CompilerParams(vmem_limit_bytes=SPLIT_LIMIT),
        cost_estimate=pl.CostEstimate(
            flops=0, bytes_accessed=8 * rows * HEAD_DIM * len(wanted), transcendentals=0
        ),
        name="split_early",
    )(*arrays, *after)


def split_rest_kernel(members, groups, *refs):
    held = refs[:4]
    own, late = refs[4], refs[5:]
    rows = held[0].shape[0]
    half = rows // 2
    fill_pack(own, held, slice(0, half), chip_column(members, groups, 0))
    for s in range(groups):
        fill_pack(late[s], held, slice(half, rows), chip_column(members, groups, s))
        late[s][rows:, :] = jnp.zeros_like(late[s][rows:, :])


def split_heads(arrays, members, groups):
    rows, width = arrays[0].shape
    out = jax.ShapeDtypeStruct((rows, 2 * HEAD_DIM), jnp.bfloat16)
    longer = jax.ShapeDtypeStruct((rows + LATE_PAD, 2 * HEAD_DIM), jnp.bfloat16)
    vmem = pl.BlockSpec(memory_space=pltpu.VMEM)
    early = split_early((1,), arrays, [], members, groups)
    early += split_early(tuple(range(2, groups)), arrays, early, members, groups)
    own, *late = pl.pallas_call(
        functools.partial(split_rest_kernel, members, groups),
        out_shape=[out] + [longer] * groups,
        in_specs=[vmem] * 4,
        out_specs=[vmem] * (groups + 1),
        compiler_params=pltpu.CompilerParams(vmem_limit_bytes=SMALL_LIMIT),
        cost_estimate=pl.CostEstimate(
            flops=0, bytes_accessed=8 * rows * width, transcendentals=0
        ),
        name="split_rest",
    )(*arrays)
    return [own, *early], late


def pairs_kernel(groups, *refs):
    outs = refs[-(groups // 2) :]
    for s in range(groups):
        out = outs[s // 2]
        out[s % 2] = refs[s][: out.shape[1], :]


def only_pairs(packs, half, after, groups):
    hbm = pl.BlockSpec(memory_space=pl.ANY)
    vmem = pl.BlockSpec(memory_space=pltpu.VMEM)
    outs = groups // 2
    return pl.pallas_call(
        functools.partial(pairs_kernel, groups),
        out_shape=[jax.ShapeDtypeStruct((2, half, 2 * HEAD_DIM), jnp.bfloat16)] * outs,
        in_specs=[vmem] * groups + [hbm] * len(after),
        out_specs=[vmem] * outs,
        compiler_params=pltpu.CompilerParams(vmem_limit_bytes=SMALL_LIMIT),
        cost_estimate=pl.CostEstimate(
            flops=0, bytes_accessed=8 * groups * half * HEAD_DIM, transcendentals=0
        ),
        name="only_pairs",
    )(*packs, *after)


def join_queries_kernel(members, groups, *refs):
    out, token = refs[-2:]
    token[...] = jnp.zeros_like(token)
    for s in range(groups):
        column = chip_column(members, groups, s)
        for n in range(out.shape[0] // BLK):
            packed = slice(n // 2 * BLK, (n // 2 + 1) * BLK)
            lanes = slice(n % 2 * HEAD_DIM, (n % 2 + 1) * HEAD_DIM)
            out[n * BLK : (n + 1) * BLK, column] = refs[s][packed, lanes]


def join_pairs_kernel(members, groups, *refs):
    outs, held, sems = refs[-5:-3], refs[-3:-1], refs[-1]
    half = refs[0].shape[0]
    copies = []
    for h in range(2):
        at = pl.ds(h * half, half)
        for t in range(2):
            lanes = slice(t * HEAD_DIM, (t + 1) * HEAD_DIM)
            for s in range(groups):
                column = chip_column(members, groups, s)
                held[t][at, column] = refs[h * groups + s][:, lanes]
            copy = pltpu.make_async_copy(held[t].at[at], outs[t].at[at], sems.at[2 * h + t])
            copy.start()
            copies.append(copy)
    for copy in copies:
        copy.wait()


def join_heads(dqs, pairs, members, groups):
    rows = 2 * pairs[0].shape[0]
    vmem = pl.BlockSpec(memory_space=pltpu.VMEM)
    out = jax.ShapeDtypeStruct((rows, groups * HEAD_DIM), jnp.bfloat16)
    token = jax.ShapeDtypeStruct((8, HEAD_DIM), jnp.float32)
    bytes_out = 2 * rows * groups * HEAD_DIM
    query_grad, token = pl.pallas_call(
        functools.partial(join_queries_kernel, members, groups),
        out_shape=[out, token],
        in_specs=[vmem] * groups,
        out_specs=[vmem] * 2,
        compiler_params=pltpu.CompilerParams(vmem_limit_bytes=SMALL_LIMIT),
        cost_estimate=pl.CostEstimate(
            flops=0, bytes_accessed=200 * bytes_out, transcendentals=0
        ),
        name="join_queries",
    )(*dqs)
    key_grad, value_grad = pl.pallas_call(
        functools.partial(join_pairs_kernel, members, groups),
        out_shape=[out] * 2,
        in_specs=[vmem] * (2 * groups + 1),
        out_specs=[pl.BlockSpec(memory_space=pl.ANY)] * 2,
        scratch_shapes=[pltpu.VMEM(out.shape, out.dtype)] * 2 + [pltpu.SemaphoreType.DMA((4,))],
        compiler_params=pltpu.CompilerParams(vmem_limit_bytes=SMALL_LIMIT),
        cost_estimate=pl.CostEstimate(flops=0, bytes_accessed=4 * bytes_out, transcendentals=0),
        name="join_pairs",
    )(*pairs, token)
    return query_grad, key_grad, value_grad


def add_kernel(members, groups, *refs):
    far = refs[: members - 1]
    own = refs[members - 1 : members - 1 + groups]
    outs = refs[members - 1 + groups :]
    half = outs[0].shape[0]
    for h in range(2):
        at = slice(h * half, (h + 1) * half)
        for s in range(groups):
            total = own[s][at, :].astype(jnp.float32)
            for part in far:
                total = total + part[s, at, :].astype(jnp.float32)
            out = outs[h * groups + s]
            out[:, :HEAD_DIM] = (total[:, :HEAD_DIM] * HEAD_DIM**-0.5).astype(jnp.bfloat16)
            out[:, HEAD_DIM:] = total[:, HEAD_DIM:].astype(jnp.bfloat16)


def add_partials(far, own, members, groups):
    vmem = pl.BlockSpec(memory_space=pltpu.VMEM)
    rows = own[0].shape[0]
    out = jax.ShapeDtypeStruct((rows // 2, 2 * HEAD_DIM), jnp.bfloat16)
    found = pl.pallas_call(
        functools.partial(add_kernel, members, groups),
        out_shape=[out] * (2 * groups),
        in_specs=[vmem] * (members - 1 + groups),
        out_specs=[vmem] * (2 * groups),
        compiler_params=pltpu.CompilerParams(vmem_limit_bytes=SMALL_LIMIT),
        cost_estimate=pl.CostEstimate(
            flops=0, bytes_accessed=8 * groups * own[0].size, transcendentals=0
        ),
        name="add_partials",
    )(*far, *own)
    return found[:groups], found[groups:]


def dot(left, right, dims):
    return lax.dot_general(left, right, (dims, ((), ())), preferred_element_type=jnp.float32)


def attend_kernel(late, near, shards, members, groups, half, *refs):
    slots = members * groups
    rows = 2 * half
    stretch = half // BLK
    links = refs[0]
    packs = [*refs[1 : 1 + groups]]
    lent = (members - 1) * (groups // 2)
    for part in refs[1 + groups : 1 + groups + lent]:
        packs += [part.at[n] for n in range(2)]
    refs = refs[1 + groups + lent :]
    if late:
        dq_early = refs[:groups]
        refs = refs[groups + 2 :]
        dq_outs = refs[:groups]
        own_outs = refs[groups : 2 * groups]
        far_outs = refs[2 * groups : 2 * groups + members - 1]
        refs = refs[2 * groups + members - 1 :]
    else:
        dq_outs = refs[:groups]
        refs = refs[groups:]
    pair_buf, acc, ask_buf, dq_buf, sems = refs
    device = lax.axis_index("ctx")

    moves = []
    for s in range(groups):
        moves.append((packs[s].at[pl.ds(half, half)], ask_buf.at[pl.ds(s * half, half)]))
        for r in range(members):
            i = r * groups + s
            place = pl.ds(i * rows + (half if late else 0), half)
            moves.append((packs[i].at[pl.ds(0, half)], pair_buf.at[place]))
    by_copy = 0 if near else len(moves)
    copies = all_started(moves[:by_copy], sems)
    for source, target in moves[by_copy:]:
        target[...] = source[...]
    if not late:
        acc[...] = jnp.zeros_like(acc)
    for copy in copies:
        copy.wait()

    scaling = HEAD_DIM**-0.5
    causal = lax.broadcasted_iota(jnp.int32, (BLK, BLK), 0) <= lax.broadcasted_iota(
        jnp.int32, (BLK, BLK), 1
    )

    def place_of(block):
        run = lax.div(block, stretch)
        local = block - run * stretch
        owner = run
        if late:
            is_late = run >= shards
            owner = jnp.where(is_late, 2 * shards - 1 - run, run)
            local = local + jnp.where(is_late, stretch, 0)
        bits = owner ^ device
        slot = lax.rem(bits, members) * groups + apart(lax.div(bits, members), groups)
        return pl.multiple_of(slot * rows + local * BLK, BLK)

    def step(s, _):
        asker = device ^ (apart(s, groups) * members)
        first = (2 * shards - 1 - asker if late else asker) * stretch
        units = range(stretch)
        listed = []
        for n in units:
            block = first + n
            listed.append([block, block - 1] + [links[block, i] for i in range(LINKS)])
        places = [[place_of(jnp.maximum(j, 0)) for j in row] for row in listed]
        pairs = [jnp.concatenate([pair_buf[pl.ds(p, BLK), :] for p in row], 0) for row in places]
        asks = [
            ask_buf[pl.ds(pl.multiple_of(s * half + n * BLK, BLK), BLK), :] for n in units
        ]
        raws = [dot(pairs[n][:, :HEAD_DIM], asks[n][:, :HEAD_DIM], ((1,), (1,))) for n in units]
        dprobs = [dot(pairs[n][:, HEAD_DIM:], asks[n][:, HEAD_DIM:], ((1,), (1,))) for n in units]
        dscore_b, terms = [], []
        for n in units:
            raw = [raws[n][i * BLK : (i + 1) * BLK] for i in range(SPAN)]
            dprob = dprobs[n].reshape(SPAN, BLK, BLK)
            raw[0] = jnp.where(causal, raw[0], NEG_FILL)
            unused = [0.0] + [jnp.where(j >= 0, 0.0, NEG_FILL) for j in listed[n][1:]]
            tops = [jnp.max(raw[i], axis=0, keepdims=True) + unused[i] for i in range(SPAN)]
            top = functools.reduce(jnp.maximum, tops)
            weight = jnp.stack(
                [
                    jnp.exp((raw[i] - (top - unused[i])) * scaling)
                    for i in range(SPAN)
                ]
            )
            share = 1.0 / jnp.sum(weight, axis=(0, 1), keepdims=True)
            delta = jnp.sum(weight * dprob, axis=(0, 1), keepdims=True) * share
            prob = weight * share
            dscore = (prob * (dprob - delta)).astype(jnp.bfloat16).reshape(SPAN * BLK, BLK)
            dscore_b.append(dscore)
            prob = prob.astype(jnp.bfloat16).reshape(SPAN * BLK, BLK)
            dk = dot(dscore, asks[n][:, :HEAD_DIM], ((1,), (0,)))
            dv = dot(prob, asks[n][:, HEAD_DIM:], ((1,), (0,)))
            terms.append(jnp.concatenate([dk, dv], 1))
        dq = [dot(dscore_b[n], pairs[n][:, :HEAD_DIM], ((0,), (0,))) * scaling for n in units]
        for n in units:
            lanes = slice(n % 2 * HEAD_DIM, (n % 2 + 1) * HEAD_DIM)
            packed = pl.ds(pl.multiple_of(s * (half // 2) + n // 2 * BLK, BLK), BLK)
            dq_buf[packed, lanes] = dq[n].astype(jnp.bfloat16)
            for i, p in enumerate(places[n]):
                acc[pl.ds(p, BLK), :] += terms[n][i * BLK : (i + 1) * BLK]
        return 0

    lax.fori_loop(0, groups, step, 0, unroll=2)

    quarter = half // 2
    for s in range(groups):
        if late:
            dq_outs[s][:quarter] = dq_early[s][...]
        start = quarter if late else 0
        dq_outs[s][start : start + quarter] = dq_buf[s * quarter : (s + 1) * quarter, :]
    if late:
        for s in range(groups):
            own_outs[s][...] = acc[s * rows : (s + 1) * rows, :].astype(jnp.bfloat16)
        for r in range(1, members):
            for s in range(groups):
                start = (r * groups + s) * rows
                far_outs[r - 1][s] = acc[start : start + rows, :].astype(jnp.bfloat16)


def attend(links, packs, dq_early, buffers, rows, shards, members, groups):
    late = len(buffers) > 0
    half = rows // 2
    slots = members * groups
    blocks = groups * half // BLK
    near = slots * rows <= 4096

    def shape(*dims, dtype=jnp.bfloat16):
        return jax.ShapeDtypeStruct((*dims, 2 * HEAD_DIM), dtype)

    outs = [shape(half if late else half // 2)] * groups
    if late:
        outs += [shape(rows)] * groups + [shape(groups, rows)] * (members - 1)
    outs += [shape(slots * rows), shape(slots * rows, dtype=jnp.float32)]
    vmem = pl.BlockSpec(memory_space=pltpu.VMEM)
    read = vmem if near else pl.BlockSpec(memory_space=pl.ANY)
    given = [*packs, *dq_early, *buffers]
    found = pl.pallas_call(
        functools.partial(attend_kernel, late, near, shards, members, groups, half),
        out_shape=outs,
        in_specs=[pl.BlockSpec(memory_space=pltpu.SMEM)]
        + [read] * len(packs)
        + [vmem] * (len(dq_early) + len(buffers)),
        out_specs=[vmem] * len(outs),
        input_output_aliases={len(given) - 1: len(outs) - 2, len(given): len(outs) - 1}
        if late
        else {},
        scratch_shapes=[
            pltpu.VMEM((groups * half, 2 * HEAD_DIM), jnp.bfloat16),
            pltpu.VMEM((groups * half // 2, 2 * HEAD_DIM), jnp.bfloat16),
            pltpu.SemaphoreType.DMA((slots + groups,)),
        ],
        compiler_params=pltpu.CompilerParams(vmem_limit_bytes=SMALL_LIMIT),
        cost_estimate=pl.CostEstimate(
            flops=10 * blocks * SPAN * BLK * BLK * HEAD_DIM if late else 0,
            bytes_accessed=8 * slots * rows * HEAD_DIM if late else 0,
            transcendentals=blocks * SPAN * BLK * BLK if late else 0,
        ),
        name="attend_late" if late else "attend_early",
    )(links, *given)
    if late:
        return found[:groups], found[groups : 2 * groups], found[2 * groups : -2]
    return found[:groups], found[-2:]


def to_chips(parts, members):
    groups = len(parts)
    return [swapped(part, -s % groups * members) if s else part for s, part in enumerate(parts)]


def with_members(parts, members):
    return [swapped(part, r) for r in range(1, members) for part in parts]


def per_device(query, key, value, out_grad, links):
    rows, width = query.shape
    groups = width // HEAD_DIM
    shards = lax.axis_size("ctx")
    members = shards // groups
    arrays = (query, key, value, out_grad)

    early, late = split_heads(arrays, members, groups)
    early = to_chips(early, members)
    late = to_chips(late, members)
    early = early + with_members(only_pairs(early, rows // 2, [], groups), members)
    dq_early, buffers = attend(links, early, [], [], rows, shards, members, groups)
    late = late + with_members(only_pairs(late, rows // 2, dq_early[:1], groups), members)
    dqs, own, far = attend(links, late, dq_early, buffers, rows, shards, members, groups)
    far = [swapped(part, r) for r, part in enumerate(far, 1)]
    dqs = to_chips(dqs, members)
    pairs = add_partials(far, own, members, groups)
    pairs = to_chips(pairs[0], members) + to_chips(pairs[1], members)
    return join_heads(dqs, pairs, members, groups)


def solution(mesh):
    return jax.shard_map(
        per_device,
        mesh=mesh,
        in_specs=(P("ctx", "head"), P("ctx", "head"), P("ctx", "head"), P("ctx", "head"), P()),
        out_specs=(P("ctx", "head"), P("ctx", "head"), P("ctx", "head")),
        check_vma=False,
    )
```

```python
import functools

import jax
import jax.numpy as jnp
from jax import lax
from jax.experimental import pallas as pl
from jax.experimental.pallas import tpu as pltpu
from jax.sharding import PartitionSpec as P

HEAD_DIM = 128
BLK = 128
WIN = 2
LINKS = 6
SPAN = WIN + LINKS
NEG_FILL = -1e30
LATE_PAD = 16
SPLIT_LIMIT = 56 * 1024 * 1024
SMALL_LIMIT = 16 * 1024 * 1024


def swapped(x, by):
    count = lax.axis_size("ctx")
    return lax.ppermute(x, "ctx", [(i, i ^ by) for i in range(count)])


def apart(s, groups):
    return lax.rem(groups - s, groups)


def chip_column(members, groups, s):
    chip = lax.div(lax.axis_index("ctx"), members)
    return pl.ds(pl.multiple_of((chip ^ (-s % groups)) * HEAD_DIM, HEAD_DIM), HEAD_DIM)


def all_started(moves, sems):
    copies = [
        pltpu.make_async_copy(source, target, sems.at[i])
        for i, (source, target) in enumerate(moves)
    ]
    for copy in copies:
        copy.start()
    return copies


def fill_pack(out, held, at, column):
    query, key, value, grad = held
    half = at.stop - at.start
    for t, (pair, ask) in enumerate(((key, query), (value, grad))):
        lanes = slice(t * HEAD_DIM, (t + 1) * HEAD_DIM)
        out[:half, lanes] = pair[at, column]
        out[half : 2 * half, lanes] = ask[at, column]


def split_early_kernel(members, groups, wanted, *refs):
    outs = refs[-1 - len(wanted) : -1]
    half = outs[0].shape[0] // 2
    rows = pl.ds(0, half)
    query, key, value, grad = refs[:4]
    moves = []
    for s, out in zip(wanted, outs):
        column = chip_column(members, groups, s)
        for t, (pair, ask) in enumerate(((key, query), (value, grad))):
            lanes = pl.ds(t * HEAD_DIM, HEAD_DIM)
            moves.append((pair.at[rows, column], out.at[rows, lanes]))
            moves.append((ask.at[rows, column], out.at[pl.ds(half, half), lanes]))
    for copy in all_started(moves, refs[-1]):
        copy.wait()


def split_early(wanted, arrays, after, members, groups):
    rows = arrays[0].shape[0]
    out = jax.ShapeDtypeStruct((rows, 2 * HEAD_DIM), jnp.bfloat16)
    return pl.pallas_call(
        functools.partial(split_early_kernel, members, groups, wanted),
        out_shape=[out] * len(wanted),
        in_specs=[pl.BlockSpec(memory_space=pl.ANY)] * (len(arrays) + len(after)),
        out_specs=[pl.BlockSpec(memory_space=pltpu.VMEM)] * len(wanted),
        scratch_shapes=[pltpu.SemaphoreType.DMA((4 * len(wanted),))],
        compiler_params=pltpu.CompilerParams(vmem_limit_bytes=SPLIT_LIMIT),
        cost_estimate=pl.CostEstimate(
            flops=0, bytes_accessed=8 * rows * HEAD_DIM * len(wanted), transcendentals=0
        ),
        name="split_early",
    )(*arrays, *after)


def split_rest_kernel(members, groups, *refs):
    held = refs[:4]
    own, late = refs[4], refs[5:]
    rows = held[0].shape[0]
    half = rows // 2
    fill_pack(own, held, slice(0, half), chip_column(members, groups, 0))
    for s in range(groups):
        fill_pack(late[s], held, slice(half, rows), chip_column(members, groups, s))
        late[s][rows:, :] = jnp.zeros_like(late[s][rows:, :])


def split_heads(arrays, members, groups):
    rows, width = arrays[0].shape
    out = jax.ShapeDtypeStruct((rows, 2 * HEAD_DIM), jnp.bfloat16)
    longer = jax.ShapeDtypeStruct((rows + LATE_PAD, 2 * HEAD_DIM), jnp.bfloat16)
    vmem = pl.BlockSpec(memory_space=pltpu.VMEM)
    early = split_early((1,), arrays, [], members, groups)
    early += split_early(tuple(range(2, groups)), arrays, early, members, groups)
    own, *late = pl.pallas_call(
        functools.partial(split_rest_kernel, members, groups),
        out_shape=[out] + [longer] * groups,
        in_specs=[vmem] * 4,
        out_specs=[vmem] * (groups + 1),
        compiler_params=pltpu.CompilerParams(vmem_limit_bytes=SMALL_LIMIT),
        cost_estimate=pl.CostEstimate(
            flops=0, bytes_accessed=8 * rows * width, transcendentals=0
        ),
        name="split_rest",
    )(*arrays)
    return [own, *early], late


def pairs_kernel(groups, *refs):
    outs = refs[-(groups // 2) :]
    for s in range(groups):
        out = outs[s // 2]
        out[s % 2] = refs[s][: out.shape[1], :]


def only_pairs(packs, half, after, groups):
    hbm = pl.BlockSpec(memory_space=pl.ANY)
    vmem = pl.BlockSpec(memory_space=pltpu.VMEM)
    outs = groups // 2
    return pl.pallas_call(
        functools.partial(pairs_kernel, groups),
        out_shape=[jax.ShapeDtypeStruct((2, half, 2 * HEAD_DIM), jnp.bfloat16)] * outs,
        in_specs=[vmem] * groups + [hbm] * len(after),
        out_specs=[vmem] * outs,
        compiler_params=pltpu.CompilerParams(vmem_limit_bytes=SMALL_LIMIT),
        cost_estimate=pl.CostEstimate(
            flops=0, bytes_accessed=8 * groups * half * HEAD_DIM, transcendentals=0
        ),
        name="only_pairs",
    )(*packs, *after)


def join_queries_kernel(members, groups, *refs):
    out, token = refs[-2:]
    token[...] = jnp.zeros_like(token)
    for s in range(groups):
        column = chip_column(members, groups, s)
        for n in range(out.shape[0] // BLK):
            packed = slice(n // 2 * BLK, (n // 2 + 1) * BLK)
            lanes = slice(n % 2 * HEAD_DIM, (n % 2 + 1) * HEAD_DIM)
            out[n * BLK : (n + 1) * BLK, column] = refs[s][packed, lanes]


def join_pairs_kernel(members, groups, *refs):
    outs, held, sems = refs[-5:-3], refs[-3:-1], refs[-1]
    half = refs[0].shape[0]
    copies = []
    for h in range(2):
        at = pl.ds(h * half, half)
        for t in range(2):
            lanes = slice(t * HEAD_DIM, (t + 1) * HEAD_DIM)
            for s in range(groups):
                column = chip_column(members, groups, s)
                held[t][at, column] = refs[h * groups + s][:, lanes]
            copy = pltpu.make_async_copy(held[t].at[at], outs[t].at[at], sems.at[2 * h + t])
            copy.start()
            copies.append(copy)
    for copy in copies:
        copy.wait()


def join_heads(dqs, pairs, members, groups):
    rows = 2 * pairs[0].shape[0]
    vmem = pl.BlockSpec(memory_space=pltpu.VMEM)
    out = jax.ShapeDtypeStruct((rows, groups * HEAD_DIM), jnp.bfloat16)
    token = jax.ShapeDtypeStruct((8, HEAD_DIM), jnp.float32)
    bytes_out = 2 * rows * groups * HEAD_DIM
    query_grad, token = pl.pallas_call(
        functools.partial(join_queries_kernel, members, groups),
        out_shape=[out, token],
        in_specs=[vmem] * groups,
        out_specs=[vmem] * 2,
        compiler_params=pltpu.CompilerParams(vmem_limit_bytes=SMALL_LIMIT),
        cost_estimate=pl.CostEstimate(
            flops=0, bytes_accessed=200 * bytes_out, transcendentals=0
        ),
        name="join_queries",
    )(*dqs)
    key_grad, value_grad = pl.pallas_call(
        functools.partial(join_pairs_kernel, members, groups),
        out_shape=[out] * 2,
        in_specs=[vmem] * (2 * groups + 1),
        out_specs=[pl.BlockSpec(memory_space=pl.ANY)] * 2,
        scratch_shapes=[pltpu.VMEM(out.shape, out.dtype)] * 2 + [pltpu.SemaphoreType.DMA((4,))],
        compiler_params=pltpu.CompilerParams(vmem_limit_bytes=SMALL_LIMIT),
        cost_estimate=pl.CostEstimate(flops=0, bytes_accessed=4 * bytes_out, transcendentals=0),
        name="join_pairs",
    )(*pairs, token)
    return query_grad, key_grad, value_grad


def add_kernel(members, groups, *refs):
    far = refs[: members - 1]
    own = refs[members - 1 : members - 1 + groups]
    outs = refs[members - 1 + groups :]
    half = outs[0].shape[0]
    for h in range(2):
        at = slice(h * half, (h + 1) * half)
        for s in range(groups):
            total = own[s][at, :].astype(jnp.float32)
            for part in far:
                total = total + part[s, at, :].astype(jnp.float32)
            out = outs[h * groups + s]
            out[:, :HEAD_DIM] = (total[:, :HEAD_DIM] * HEAD_DIM**-0.5).astype(jnp.bfloat16)
            out[:, HEAD_DIM:] = total[:, HEAD_DIM:].astype(jnp.bfloat16)


def add_partials(far, own, members, groups):
    vmem = pl.BlockSpec(memory_space=pltpu.VMEM)
    rows = own[0].shape[0]
    out = jax.ShapeDtypeStruct((rows // 2, 2 * HEAD_DIM), jnp.bfloat16)
    found = pl.pallas_call(
        functools.partial(add_kernel, members, groups),
        out_shape=[out] * (2 * groups),
        in_specs=[vmem] * (members - 1 + groups),
        out_specs=[vmem] * (2 * groups),
        compiler_params=pltpu.CompilerParams(vmem_limit_bytes=SMALL_LIMIT),
        cost_estimate=pl.CostEstimate(
            flops=0, bytes_accessed=8 * groups * own[0].size, transcendentals=0
        ),
        name="add_partials",
    )(*far, *own)
    return found[:groups], found[groups:]


def dot(left, right, dims):
    return lax.dot_general(left, right, (dims, ((), ())), preferred_element_type=jnp.float32)


def attend_kernel(late, near, shards, members, groups, half, *refs):
    slots = members * groups
    rows = 2 * half
    stretch = half // BLK
    links = refs[0]
    packs = [*refs[1 : 1 + groups]]
    lent = (members - 1) * (groups // 2)
    for part in refs[1 + groups : 1 + groups + lent]:
        packs += [part.at[n] for n in range(2)]
    refs = refs[1 + groups + lent :]
    if late:
        dq_early = refs[:groups]
        refs = refs[groups + 2 :]
        dq_outs = refs[:groups]
        own_outs = refs[groups : 2 * groups]
        far_outs = refs[2 * groups : 2 * groups + members - 1]
        refs = refs[2 * groups + members - 1 :]
    else:
        dq_outs = refs[:groups]
        refs = refs[groups:]
    pair_buf, acc, ask_buf, dq_buf, sems = refs
    device = lax.axis_index("ctx")

    moves = []
    for s in range(groups):
        moves.append((packs[s].at[pl.ds(half, half)], ask_buf.at[pl.ds(s * half, half)]))
        for r in range(members):
            i = r * groups + s
            place = pl.ds(i * rows + (half if late else 0), half)
            moves.append((packs[i].at[pl.ds(0, half)], pair_buf.at[place]))
    by_copy = 0 if near else len(moves)
    copies = all_started(moves[:by_copy], sems)
    for source, target in moves[by_copy:]:
        target[...] = source[...]
    if not late:
        acc[...] = jnp.zeros_like(acc)
    for copy in copies:
        copy.wait()

    scaling = HEAD_DIM**-0.5
    causal = lax.broadcasted_iota(jnp.int32, (BLK, BLK), 0) <= lax.broadcasted_iota(
        jnp.int32, (BLK, BLK), 1
    )

    def place_of(block):
        run = lax.div(block, stretch)
        local = block - run * stretch
        owner = run
        if late:
            is_late = run >= shards
            owner = jnp.where(is_late, 2 * shards - 1 - run, run)
            local = local + jnp.where(is_late, stretch, 0)
        bits = owner ^ device
        slot = lax.rem(bits, members) * groups + apart(lax.div(bits, members), groups)
        return pl.multiple_of(slot * rows + local * BLK, BLK)

    def step(s, _):
        asker = device ^ (apart(s, groups) * members)
        first = (2 * shards - 1 - asker if late else asker) * stretch
        units = range(stretch)
        listed = []
        for n in units:
            block = first + n
            listed.append([block, block - 1] + [links[block, i] for i in range(LINKS)])
        places = [[place_of(jnp.maximum(j, 0)) for j in row] for row in listed]
        pairs = [jnp.concatenate([pair_buf[pl.ds(p, BLK), :] for p in row], 0) for row in places]
        asks = [
            ask_buf[pl.ds(pl.multiple_of(s * half + n * BLK, BLK), BLK), :] for n in units
        ]
        raws = [dot(pairs[n][:, :HEAD_DIM], asks[n][:, :HEAD_DIM], ((1,), (1,))) for n in units]
        dprobs = [dot(pairs[n][:, HEAD_DIM:], asks[n][:, HEAD_DIM:], ((1,), (1,))) for n in units]
        dscore_b, terms = [], []
        for n in units:
            raw = [raws[n][i * BLK : (i + 1) * BLK] for i in range(SPAN)]
            dprob = dprobs[n].reshape(SPAN, BLK, BLK)
            raw[0] = jnp.where(causal, raw[0], NEG_FILL)
            unused = [0.0] + [jnp.where(j >= 0, 0.0, NEG_FILL) for j in listed[n][1:]]
            tops = [jnp.max(raw[i], axis=0, keepdims=True) + unused[i] for i in range(SPAN)]
            top = functools.reduce(jnp.maximum, tops)
            weight = jnp.stack(
                [
                    jnp.exp((raw[i] - (top - unused[i])) * scaling)
                    for i in range(SPAN)
                ]
            )
            share = 1.0 / jnp.sum(weight, axis=(0, 1), keepdims=True)
            delta = jnp.sum(weight * dprob, axis=(0, 1), keepdims=True) * share
            prob = weight * share
            dscore = (prob * (dprob - delta)).astype(jnp.bfloat16).reshape(SPAN * BLK, BLK)
            dscore_b.append(dscore)
            prob = prob.astype(jnp.bfloat16).reshape(SPAN * BLK, BLK)
            dk = dot(dscore, asks[n][:, :HEAD_DIM], ((1,), (0,)))
            dv = dot(prob, asks[n][:, HEAD_DIM:], ((1,), (0,)))
            terms.append(jnp.concatenate([dk, dv], 1))
        dq = [dot(dscore_b[n], pairs[n][:, :HEAD_DIM], ((0,), (0,))) * scaling for n in units]
        for n in units:
            lanes = slice(n % 2 * HEAD_DIM, (n % 2 + 1) * HEAD_DIM)
            packed = pl.ds(pl.multiple_of(s * (half // 2) + n // 2 * BLK, BLK), BLK)
            dq_buf[packed, lanes] = dq[n].astype(jnp.bfloat16)
            for i, p in enumerate(places[n]):
                acc[pl.ds(p, BLK), :] += terms[n][i * BLK : (i + 1) * BLK]
        return 0

    lax.fori_loop(0, groups, step, 0, unroll=4)

    quarter = half // 2
    for s in range(groups):
        if late:
            dq_outs[s][:quarter] = dq_early[s][...]
        start = quarter if late else 0
        dq_outs[s][start : start + quarter] = dq_buf[s * quarter : (s + 1) * quarter, :]
    if late:
        for s in range(groups):
            own_outs[s][...] = acc[s * rows : (s + 1) * rows, :].astype(jnp.bfloat16)
        for r in range(1, members):
            for s in range(groups):
                start = (r * groups + s) * rows
                far_outs[r - 1][s] = acc[start : start + rows, :].astype(jnp.bfloat16)


def attend(links, packs, dq_early, buffers, rows, shards, members, groups):
    late = len(buffers) > 0
    half = rows // 2
    slots = members * groups
    blocks = groups * half // BLK
    near = slots * rows <= 4096

    def shape(*dims, dtype=jnp.bfloat16):
        return jax.ShapeDtypeStruct((*dims, 2 * HEAD_DIM), dtype)

    outs = [shape(half if late else half // 2)] * groups
    if late:
        outs += [shape(rows)] * groups + [shape(groups, rows)] * (members - 1)
    outs += [shape(slots * rows), shape(slots * rows, dtype=jnp.float32)]
    vmem = pl.BlockSpec(memory_space=pltpu.VMEM)
    read = vmem if near else pl.BlockSpec(memory_space=pl.ANY)
    given = [*packs, *dq_early, *buffers]
    found = pl.pallas_call(
        functools.partial(attend_kernel, late, near, shards, members, groups, half),
        out_shape=outs,
        in_specs=[pl.BlockSpec(memory_space=pltpu.SMEM)]
        + [read] * len(packs)
        + [vmem] * (len(dq_early) + len(buffers)),
        out_specs=[vmem] * len(outs),
        input_output_aliases={len(given) - 1: len(outs) - 2, len(given): len(outs) - 1}
        if late
        else {},
        scratch_shapes=[
            pltpu.VMEM((groups * half, 2 * HEAD_DIM), jnp.bfloat16),
            pltpu.VMEM((groups * half // 2, 2 * HEAD_DIM), jnp.bfloat16),
            pltpu.SemaphoreType.DMA((slots + groups,)),
        ],
        compiler_params=pltpu.CompilerParams(vmem_limit_bytes=SMALL_LIMIT),
        cost_estimate=pl.CostEstimate(
            flops=10 * blocks * SPAN * BLK * BLK * HEAD_DIM if late else 0,
            bytes_accessed=8 * slots * rows * HEAD_DIM if late else 0,
            transcendentals=blocks * SPAN * BLK * BLK if late else 0,
        ),
        name="attend_late" if late else "attend_early",
    )(links, *given)
    if late:
        return found[:groups], found[groups : 2 * groups], found[2 * groups : -2]
    return found[:groups], found[-2:]


def to_chips(parts, members):
    groups = len(parts)
    return [swapped(part, -s % groups * members) if s else part for s, part in enumerate(parts)]


def with_members(parts, members):
    return [swapped(part, r) for r in range(1, members) for part in parts]


def per_device(query, key, value, out_grad, links):
    rows, width = query.shape
    groups = width // HEAD_DIM
    shards = lax.axis_size("ctx")
    members = shards // groups
    arrays = (query, key, value, out_grad)

    early, late = split_heads(arrays, members, groups)
    early = to_chips(early, members)
    late = to_chips(late, members)
    early = early + with_members(only_pairs(early, rows // 2, [], groups), members)
    dq_early, buffers = attend(links, early, [], [], rows, shards, members, groups)
    lent = []
    for s in range(0, groups, 2):
        lent += only_pairs(late[s : s + 2], rows // 2, dq_early[:1], 2)
    late = late + with_members(lent, members)
    dqs, own, far = attend(links, late, dq_early, buffers, rows, shards, members, groups)
    far = [swapped(part, r) for r, part in enumerate(far, 1)]
    dqs = to_chips(dqs, members)
    pairs = add_partials(far, own, members, groups)
    pairs = to_chips(pairs[0], members) + to_chips(pairs[1], members)
    return join_heads(dqs, pairs, members, groups)


def solution(mesh):
    return jax.shard_map(
        per_device,
        mesh=mesh,
        in_specs=(P("ctx", "head"), P("ctx", "head"), P("ctx", "head"), P("ctx", "head"), P()),
        out_specs=(P("ctx", "head"), P("ctx", "head"), P("ctx", "head")),
        check_vma=False,
    )
```

```python
import functools

import jax
import jax.numpy as jnp
from jax import lax
from jax.experimental import pallas as pl
from jax.experimental.pallas import tpu as pltpu
from jax.sharding import PartitionSpec as P

HEAD_DIM = 128
BLK = 128
WIN = 2
LINKS = 6
SPAN = WIN + LINKS
NEG_FILL = -1e30
LATE_PAD = 16
SPLIT_LIMIT = 56 * 1024 * 1024
SMALL_LIMIT = 16 * 1024 * 1024


def swapped(x, by):
    count = lax.axis_size("ctx")
    return lax.ppermute(x, "ctx", [(i, i ^ by) for i in range(count)])


def apart(s, groups):
    return lax.rem(groups - s, groups)


def chip_column(members, groups, s):
    chip = lax.div(lax.axis_index("ctx"), members)
    return pl.ds(pl.multiple_of((chip ^ (-s % groups)) * HEAD_DIM, HEAD_DIM), HEAD_DIM)


def all_started(moves, sems):
    copies = [
        pltpu.make_async_copy(source, target, sems.at[i])
        for i, (source, target) in enumerate(moves)
    ]
    for copy in copies:
        copy.start()
    return copies


def fill_pack(out, held, at, column):
    query, key, value, grad = held
    half = at.stop - at.start
    for t, (pair, ask) in enumerate(((key, query), (value, grad))):
        lanes = slice(t * HEAD_DIM, (t + 1) * HEAD_DIM)
        out[:half, lanes] = pair[at, column]
        out[half : 2 * half, lanes] = ask[at, column]


def split_early_kernel(members, groups, wanted, *refs):
    outs = refs[-1 - len(wanted) : -1]
    half = outs[0].shape[0] // 2
    rows = pl.ds(0, half)
    query, key, value, grad = refs[:4]
    moves = []
    for s, out in zip(wanted, outs):
        column = chip_column(members, groups, s)
        for t, (pair, ask) in enumerate(((key, query), (value, grad))):
            lanes = pl.ds(t * HEAD_DIM, HEAD_DIM)
            moves.append((pair.at[rows, column], out.at[rows, lanes]))
            moves.append((ask.at[rows, column], out.at[pl.ds(half, half), lanes]))
    for copy in all_started(moves, refs[-1]):
        copy.wait()


def split_early(wanted, arrays, after, members, groups):
    rows = arrays[0].shape[0]
    out = jax.ShapeDtypeStruct((rows, 2 * HEAD_DIM), jnp.bfloat16)
    return pl.pallas_call(
        functools.partial(split_early_kernel, members, groups, wanted),
        out_shape=[out] * len(wanted),
        in_specs=[pl.BlockSpec(memory_space=pl.ANY)] * (len(arrays) + len(after)),
        out_specs=[pl.BlockSpec(memory_space=pltpu.VMEM)] * len(wanted),
        scratch_shapes=[pltpu.SemaphoreType.DMA((4 * len(wanted),))],
        compiler_params=pltpu.CompilerParams(vmem_limit_bytes=SPLIT_LIMIT),
        cost_estimate=pl.CostEstimate(
            flops=0, bytes_accessed=8 * rows * HEAD_DIM * len(wanted), transcendentals=0
        ),
        name="split_early",
    )(*arrays, *after)


def split_rest_kernel(members, groups, *refs):
    held = refs[:4]
    own, late = refs[4], refs[5:]
    rows = held[0].shape[0]
    half = rows // 2
    fill_pack(own, held, slice(0, half), chip_column(members, groups, 0))
    for s in range(groups):
        fill_pack(late[s], held, slice(half, rows), chip_column(members, groups, s))
        late[s][rows:, :] = jnp.zeros_like(late[s][rows:, :])


def split_heads(arrays, members, groups):
    rows, width = arrays[0].shape
    out = jax.ShapeDtypeStruct((rows, 2 * HEAD_DIM), jnp.bfloat16)
    longer = jax.ShapeDtypeStruct((rows + LATE_PAD, 2 * HEAD_DIM), jnp.bfloat16)
    vmem = pl.BlockSpec(memory_space=pltpu.VMEM)
    early = split_early((1,), arrays, [], members, groups)
    early += split_early(tuple(range(2, groups)), arrays, early, members, groups)
    own, *late = pl.pallas_call(
        functools.partial(split_rest_kernel, members, groups),
        out_shape=[out] + [longer] * groups,
        in_specs=[vmem] * 4,
        out_specs=[vmem] * (groups + 1),
        compiler_params=pltpu.CompilerParams(vmem_limit_bytes=SMALL_LIMIT),
        cost_estimate=pl.CostEstimate(
            flops=0, bytes_accessed=8 * rows * width, transcendentals=0
        ),
        name="split_rest",
    )(*arrays)
    return [own, *early], late


def pairs_kernel(groups, *refs):
    outs = refs[-(groups // 2) :]
    for s in range(groups):
        out = outs[s // 2]
        out[s % 2] = refs[s][: out.shape[1], :]


def only_pairs(packs, half, after, groups):
    hbm = pl.BlockSpec(memory_space=pl.ANY)
    vmem = pl.BlockSpec(memory_space=pltpu.VMEM)
    outs = groups // 2
    return pl.pallas_call(
        functools.partial(pairs_kernel, groups),
        out_shape=[jax.ShapeDtypeStruct((2, half, 2 * HEAD_DIM), jnp.bfloat16)] * outs,
        in_specs=[vmem] * groups + [hbm] * len(after),
        out_specs=[vmem] * outs,
        compiler_params=pltpu.CompilerParams(vmem_limit_bytes=SMALL_LIMIT),
        cost_estimate=pl.CostEstimate(
            flops=0, bytes_accessed=8 * groups * half * HEAD_DIM, transcendentals=0
        ),
        name="only_pairs",
    )(*packs, *after)


def write_half(members, groups, h, parts, outs, held, sems):
    half = held[0].shape[0]
    copies = []
    for t in range(2):
        lanes = slice(t * HEAD_DIM, (t + 1) * HEAD_DIM)
        for s in range(groups):
            held[t][:, chip_column(members, groups, s)] = parts[s][:, lanes]
        copy = pltpu.make_async_copy(held[t], outs[t].at[pl.ds(h * half, half)], sems.at[t])
        copy.start()
        copies.append(copy)
    return copies


def join_first_kernel(members, groups, *refs):
    dqs, pairs = refs[:groups], refs[groups : 2 * groups]
    out, *outs = refs[2 * groups : 2 * groups + 3]
    *held, sems = refs[2 * groups + 3 :]
    copies = write_half(members, groups, 0, pairs, outs, held, sems)
    for s in range(groups):
        column = chip_column(members, groups, s)
        for n in range(out.shape[0] // BLK):
            packed = slice(n // 2 * BLK, (n // 2 + 1) * BLK)
            lanes = slice(n % 2 * HEAD_DIM, (n % 2 + 1) * HEAD_DIM)
            out[n * BLK : (n + 1) * BLK, column] = dqs[s][packed, lanes]
    for copy in copies:
        copy.wait()


def join_second_kernel(members, groups, *refs):
    outs = refs[groups + 2 : groups + 4]
    *held, sems = refs[groups + 4 :]
    for copy in write_half(members, groups, 1, refs[:groups], outs, held, sems):
        copy.wait()


def join_heads(dqs, pairs, members, groups):
    half = pairs[0].shape[0]
    vmem = pl.BlockSpec(memory_space=pltpu.VMEM)
    hbm = pl.BlockSpec(memory_space=pl.ANY)
    out = jax.ShapeDtypeStruct((2 * half, groups * HEAD_DIM), jnp.bfloat16)
    scratch = [pltpu.VMEM((half, groups * HEAD_DIM), jnp.bfloat16)] * 2
    scratch += [pltpu.SemaphoreType.DMA((2,))]
    bytes_out = 2 * half * groups * HEAD_DIM
    query_grad, key_grad, value_grad = pl.pallas_call(
        functools.partial(join_first_kernel, members, groups),
        out_shape=[out] * 3,
        in_specs=[vmem] * (2 * groups),
        out_specs=[vmem, hbm, hbm],
        scratch_shapes=scratch,
        compiler_params=pltpu.CompilerParams(vmem_limit_bytes=SMALL_LIMIT),
        cost_estimate=pl.CostEstimate(flops=0, bytes_accessed=8 * bytes_out, transcendentals=0),
        name="join_first",
    )(*dqs, *pairs[:groups])
    key_grad, value_grad = pl.pallas_call(
        functools.partial(join_second_kernel, members, groups),
        out_shape=[out] * 2,
        in_specs=[vmem] * groups + [hbm] * 2,
        out_specs=[hbm] * 2,
        scratch_shapes=scratch,
        input_output_aliases={groups: 0, groups + 1: 1},
        compiler_params=pltpu.CompilerParams(vmem_limit_bytes=SMALL_LIMIT),
        cost_estimate=pl.CostEstimate(flops=0, bytes_accessed=4 * bytes_out, transcendentals=0),
        name="join_second",
    )(*pairs[groups:], key_grad, value_grad)
    return query_grad, key_grad, value_grad


def add_kernel(members, groups, *refs):
    far = refs[: members - 1]
    own = refs[members - 1 : members - 1 + groups]
    outs = refs[members - 1 + groups :]
    half = outs[0].shape[0]
    for h in range(2):
        at = slice(h * half, (h + 1) * half)
        for s in range(groups):
            total = own[s][at, :].astype(jnp.float32)
            for part in far:
                total = total + part[s, at, :].astype(jnp.float32)
            out = outs[h * groups + s]
            out[:, :HEAD_DIM] = (total[:, :HEAD_DIM] * HEAD_DIM**-0.5).astype(jnp.bfloat16)
            out[:, HEAD_DIM:] = total[:, HEAD_DIM:].astype(jnp.bfloat16)


def add_partials(far, own, members, groups):
    vmem = pl.BlockSpec(memory_space=pltpu.VMEM)
    rows = own[0].shape[0]
    out = jax.ShapeDtypeStruct((rows // 2, 2 * HEAD_DIM), jnp.bfloat16)
    found = pl.pallas_call(
        functools.partial(add_kernel, members, groups),
        out_shape=[out] * (2 * groups),
        in_specs=[vmem] * (members - 1 + groups),
        out_specs=[vmem] * (2 * groups),
        compiler_params=pltpu.CompilerParams(vmem_limit_bytes=SMALL_LIMIT),
        cost_estimate=pl.CostEstimate(
            flops=0, bytes_accessed=8 * groups * own[0].size, transcendentals=0
        ),
        name="add_partials",
    )(*far, *own)
    return found[:groups], found[groups:]


def dot(left, right, dims):
    return lax.dot_general(left, right, (dims, ((), ())), preferred_element_type=jnp.float32)


def attend_kernel(late, near, shards, members, groups, half, *refs):
    slots = members * groups
    rows = 2 * half
    stretch = half // BLK
    links = refs[0]
    packs = [*refs[1 : 1 + groups]]
    lent = (members - 1) * (groups // 2)
    for part in refs[1 + groups : 1 + groups + lent]:
        packs += [part.at[n] for n in range(2)]
    refs = refs[1 + groups + lent :]
    if late:
        dq_early = refs[:groups]
        refs = refs[groups + 2 :]
        dq_outs = refs[:groups]
        own_outs = refs[groups : 2 * groups]
        far_outs = refs[2 * groups : 2 * groups + members - 1]
        refs = refs[2 * groups + members - 1 :]
    else:
        dq_outs = refs[:groups]
        refs = refs[groups:]
    pair_buf, acc, ask_buf, dq_buf, sems = refs
    device = lax.axis_index("ctx")

    moves = []
    for s in range(groups):
        moves.append((packs[s].at[pl.ds(half, half)], ask_buf.at[pl.ds(s * half, half)]))
        for r in range(members):
            i = r * groups + s
            place = pl.ds(i * rows + (half if late else 0), half)
            moves.append((packs[i].at[pl.ds(0, half)], pair_buf.at[place]))
    by_copy = 0 if near else len(moves)
    copies = all_started(moves[:by_copy], sems)
    for source, target in moves[by_copy:]:
        target[...] = source[...]
    if not late:
        acc[...] = jnp.zeros_like(acc)
    for copy in copies:
        copy.wait()

    scaling = HEAD_DIM**-0.5
    causal = lax.broadcasted_iota(jnp.int32, (BLK, BLK), 0) <= lax.broadcasted_iota(
        jnp.int32, (BLK, BLK), 1
    )

    def place_of(block):
        run = lax.div(block, stretch)
        local = block - run * stretch
        owner = run
        if late:
            is_late = run >= shards
            owner = jnp.where(is_late, 2 * shards - 1 - run, run)
            local = local + jnp.where(is_late, stretch, 0)
        bits = owner ^ device
        slot = lax.rem(bits, members) * groups + apart(lax.div(bits, members), groups)
        return pl.multiple_of(slot * rows + local * BLK, BLK)

    def step(s, _):
        asker = device ^ (apart(s, groups) * members)
        first = (2 * shards - 1 - asker if late else asker) * stretch
        units = range(stretch)
        listed = []
        for n in units:
            block = first + n
            listed.append([block, block - 1] + [links[block, i] for i in range(LINKS)])
        places = [[place_of(jnp.maximum(j, 0)) for j in row] for row in listed]
        pairs = [jnp.concatenate([pair_buf[pl.ds(p, BLK), :] for p in row], 0) for row in places]
        asks = [
            ask_buf[pl.ds(pl.multiple_of(s * half + n * BLK, BLK), BLK), :] for n in units
        ]
        raws = [dot(pairs[n][:, :HEAD_DIM], asks[n][:, :HEAD_DIM], ((1,), (1,))) for n in units]
        dprobs = [dot(pairs[n][:, HEAD_DIM:], asks[n][:, HEAD_DIM:], ((1,), (1,))) for n in units]
        dscore_b, terms = [], []
        for n in units:
            raw = [raws[n][i * BLK : (i + 1) * BLK] for i in range(SPAN)]
            dprob = dprobs[n].reshape(SPAN, BLK, BLK)
            raw[0] = jnp.where(causal, raw[0], NEG_FILL)
            unused = [0.0] + [jnp.where(j >= 0, 0.0, NEG_FILL) for j in listed[n][1:]]
            tops = [jnp.max(raw[i], axis=0, keepdims=True) + unused[i] for i in range(SPAN)]
            top = functools.reduce(jnp.maximum, tops)
            weight = jnp.stack(
                [
                    jnp.exp((raw[i] - (top - unused[i])) * scaling)
                    for i in range(SPAN)
                ]
            )
            share = 1.0 / jnp.sum(weight, axis=(0, 1), keepdims=True)
            delta = jnp.sum(weight * dprob, axis=(0, 1), keepdims=True) * share
            prob = weight * share
            dscore = (prob * (dprob - delta)).astype(jnp.bfloat16).reshape(SPAN * BLK, BLK)
            dscore_b.append(dscore)
            prob = prob.astype(jnp.bfloat16).reshape(SPAN * BLK, BLK)
            dk = dot(dscore, asks[n][:, :HEAD_DIM], ((1,), (0,)))
            dv = dot(prob, asks[n][:, HEAD_DIM:], ((1,), (0,)))
            terms.append(jnp.concatenate([dk, dv], 1))
        dq = [dot(dscore_b[n], pairs[n][:, :HEAD_DIM], ((0,), (0,))) * scaling for n in units]
        for n in units:
            lanes = slice(n % 2 * HEAD_DIM, (n % 2 + 1) * HEAD_DIM)
            packed = pl.ds(pl.multiple_of(s * (half // 2) + n // 2 * BLK, BLK), BLK)
            dq_buf[packed, lanes] = dq[n].astype(jnp.bfloat16)
            for i, p in enumerate(places[n]):
                acc[pl.ds(p, BLK), :] += terms[n][i * BLK : (i + 1) * BLK]
        return 0

    lax.fori_loop(0, groups, step, 0, unroll=4)

    quarter = half // 2
    for s in range(groups):
        if late:
            dq_outs[s][:quarter] = dq_early[s][...]
        start = quarter if late else 0
        dq_outs[s][start : start + quarter] = dq_buf[s * quarter : (s + 1) * quarter, :]
    if late:
        for s in range(groups):
            own_outs[s][...] = acc[s * rows : (s + 1) * rows, :].astype(jnp.bfloat16)
        for r in range(1, members):
            for s in range(groups):
                start = (r * groups + s) * rows
                far_outs[r - 1][s] = acc[start : start + rows, :].astype(jnp.bfloat16)


def attend(links, packs, dq_early, buffers, rows, shards, members, groups):
    late = len(buffers) > 0
    half = rows // 2
    slots = members * groups
    blocks = groups * half // BLK
    near = slots * rows <= 4096

    def shape(*dims, dtype=jnp.bfloat16):
        return jax.ShapeDtypeStruct((*dims, 2 * HEAD_DIM), dtype)

    outs = [shape(half if late else half // 2)] * groups
    if late:
        outs += [shape(rows)] * groups + [shape(groups, rows)] * (members - 1)
    outs += [shape(slots * rows), shape(slots * rows, dtype=jnp.float32)]
    vmem = pl.BlockSpec(memory_space=pltpu.VMEM)
    read = vmem if near else pl.BlockSpec(memory_space=pl.ANY)
    given = [*packs, *dq_early, *buffers]
    found = pl.pallas_call(
        functools.partial(attend_kernel, late, near, shards, members, groups, half),
        out_shape=outs,
        in_specs=[pl.BlockSpec(memory_space=pltpu.SMEM)]
        + [read] * len(packs)
        + [vmem] * (len(dq_early) + len(buffers)),
        out_specs=[vmem] * len(outs),
        input_output_aliases={len(given) - 1: len(outs) - 2, len(given): len(outs) - 1}
        if late
        else {},
        scratch_shapes=[
            pltpu.VMEM((groups * half, 2 * HEAD_DIM), jnp.bfloat16),
            pltpu.VMEM((groups * half // 2, 2 * HEAD_DIM), jnp.bfloat16),
            pltpu.SemaphoreType.DMA((slots + groups,)),
        ],
        compiler_params=pltpu.CompilerParams(vmem_limit_bytes=SMALL_LIMIT),
        cost_estimate=pl.CostEstimate(
            flops=10 * blocks * SPAN * BLK * BLK * HEAD_DIM if late else 0,
            bytes_accessed=8 * slots * rows * HEAD_DIM if late else 0,
            transcendentals=blocks * SPAN * BLK * BLK if late else 0,
        ),
        name="attend_late" if late else "attend_early",
    )(links, *given)
    if late:
        return found[:groups], found[groups : 2 * groups], found[2 * groups : -2]
    return found[:groups], found[-2:]


def to_chips(parts, members):
    groups = len(parts)
    return [swapped(part, -s % groups * members) if s else part for s, part in enumerate(parts)]


def with_members(parts, members):
    return [swapped(part, r) for r in range(1, members) for part in parts]


def per_device(query, key, value, out_grad, links):
    rows, width = query.shape
    groups = width // HEAD_DIM
    shards = lax.axis_size("ctx")
    members = shards // groups
    arrays = (query, key, value, out_grad)

    early, late = split_heads(arrays, members, groups)
    early = to_chips(early, members)
    late = to_chips(late, members)
    early = early + with_members(only_pairs(early, rows // 2, [], groups), members)
    dq_early, buffers = attend(links, early, [], [], rows, shards, members, groups)
    lent = []
    for s in range(0, groups, 2):
        lent += only_pairs(late[s : s + 2], rows // 2, dq_early[:1], 2)
    late = late + with_members(lent, members)
    dqs, own, far = attend(links, late, dq_early, buffers, rows, shards, members, groups)
    far = [swapped(part, r) for r, part in enumerate(far, 1)]
    dqs = to_chips(dqs, members)
    pairs = add_partials(far, own, members, groups)
    pairs = to_chips(pairs[0], members) + to_chips(pairs[1], members)
    return join_heads(dqs, pairs, members, groups)


def solution(mesh):
    return jax.shard_map(
        per_device,
        mesh=mesh,
        in_specs=(P("ctx", "head"), P("ctx", "head"), P("ctx", "head"), P("ctx", "head"), P()),
        out_specs=(P("ctx", "head"), P("ctx", "head"), P("ctx", "head")),
        check_vma=False,
    )
```

```python
import functools

import jax
import jax.numpy as jnp
from jax import lax
from jax.experimental import pallas as pl
from jax.experimental.pallas import tpu as pltpu
from jax.sharding import PartitionSpec as P

HEAD_DIM = 128
BLK = 128
WIN = 2
LINKS = 6
SPAN = WIN + LINKS
NEG_FILL = -1e30
LATE_PAD = 16
SPLIT_LIMIT = 56 * 1024 * 1024
SMALL_LIMIT = 16 * 1024 * 1024


def swapped(x, by):
    count = lax.axis_size("ctx")
    return lax.ppermute(x, "ctx", [(i, i ^ by) for i in range(count)])


def apart(s, groups):
    return lax.rem(groups - s, groups)


def chip_column(members, groups, s):
    chip = lax.div(lax.axis_index("ctx"), members)
    return pl.ds(pl.multiple_of((chip ^ (-s % groups)) * HEAD_DIM, HEAD_DIM), HEAD_DIM)


def all_started(moves, sems):
    copies = [
        pltpu.make_async_copy(source, target, sems.at[i])
        for i, (source, target) in enumerate(moves)
    ]
    for copy in copies:
        copy.start()
    return copies


def fill_pack(out, held, at, column):
    query, key, value, grad = held
    half = at.stop - at.start
    for t, (pair, ask) in enumerate(((key, query), (value, grad))):
        lanes = slice(t * HEAD_DIM, (t + 1) * HEAD_DIM)
        out[:half, lanes] = pair[at, column]
        out[half : 2 * half, lanes] = ask[at, column]


def split_early_kernel(members, groups, wanted, *refs):
    outs = refs[-1 - len(wanted) : -1]
    half = outs[0].shape[0] // 2
    rows = pl.ds(0, half)
    query, key, value, grad = refs[:4]
    moves = []
    for s, out in zip(wanted, outs):
        column = chip_column(members, groups, s)
        for t, (pair, ask) in enumerate(((key, query), (value, grad))):
            lanes = pl.ds(t * HEAD_DIM, HEAD_DIM)
            moves.append((pair.at[rows, column], out.at[rows, lanes]))
            moves.append((ask.at[rows, column], out.at[pl.ds(half, half), lanes]))
    for copy in all_started(moves, refs[-1]):
        copy.wait()


def split_early(wanted, arrays, after, members, groups):
    rows = arrays[0].shape[0]
    out = jax.ShapeDtypeStruct((rows, 2 * HEAD_DIM), jnp.bfloat16)
    return pl.pallas_call(
        functools.partial(split_early_kernel, members, groups, wanted),
        out_shape=[out] * len(wanted),
        in_specs=[pl.BlockSpec(memory_space=pl.ANY)] * (len(arrays) + len(after)),
        out_specs=[pl.BlockSpec(memory_space=pltpu.VMEM)] * len(wanted),
        scratch_shapes=[pltpu.SemaphoreType.DMA((4 * len(wanted),))],
        compiler_params=pltpu.CompilerParams(vmem_limit_bytes=SPLIT_LIMIT),
        cost_estimate=pl.CostEstimate(
            flops=0, bytes_accessed=8 * rows * HEAD_DIM * len(wanted), transcendentals=0
        ),
        name="split_early",
    )(*arrays, *after)


def split_rest_kernel(members, groups, *refs):
    held = refs[:4]
    own, late = refs[4], refs[5:]
    rows = held[0].shape[0]
    half = rows // 2
    fill_pack(own, held, slice(0, half), chip_column(members, groups, 0))
    for s in range(groups):
        fill_pack(late[s], held, slice(half, rows), chip_column(members, groups, s))
        late[s][rows:, :] = jnp.zeros_like(late[s][rows:, :])


def split_heads(arrays, members, groups):
    rows, width = arrays[0].shape
    out = jax.ShapeDtypeStruct((rows, 2 * HEAD_DIM), jnp.bfloat16)
    longer = jax.ShapeDtypeStruct((rows + LATE_PAD, 2 * HEAD_DIM), jnp.bfloat16)
    vmem = pl.BlockSpec(memory_space=pltpu.VMEM)
    early = split_early((1,), arrays, [], members, groups)
    early += split_early(tuple(range(2, groups)), arrays, early, members, groups)
    own, *late = pl.pallas_call(
        functools.partial(split_rest_kernel, members, groups),
        out_shape=[out] + [longer] * groups,
        in_specs=[vmem] * 4,
        out_specs=[vmem] * (groups + 1),
        compiler_params=pltpu.CompilerParams(vmem_limit_bytes=SMALL_LIMIT),
        cost_estimate=pl.CostEstimate(
            flops=0, bytes_accessed=8 * rows * width, transcendentals=0
        ),
        name="split_rest",
    )(*arrays)
    return [own, *early], late


def pairs_kernel(per, outs, *refs):
    for s in range(per * outs):
        out = refs[s // per - outs]
        out[s % per] = refs[s][: out.shape[1], :]


def only_pairs(packs, half, after, per):
    hbm = pl.BlockSpec(memory_space=pl.ANY)
    vmem = pl.BlockSpec(memory_space=pltpu.VMEM)
    outs = len(packs) // per
    return pl.pallas_call(
        functools.partial(pairs_kernel, per, outs),
        out_shape=[jax.ShapeDtypeStruct((per, half, 2 * HEAD_DIM), jnp.bfloat16)] * outs,
        in_specs=[vmem] * len(packs) + [hbm] * len(after),
        out_specs=[vmem] * outs,
        compiler_params=pltpu.CompilerParams(vmem_limit_bytes=SMALL_LIMIT),
        cost_estimate=pl.CostEstimate(
            flops=0, bytes_accessed=8 * len(packs) * half * HEAD_DIM, transcendentals=0
        ),
        name="only_pairs",
    )(*packs, *after)


def write_half(members, groups, h, parts, outs, held, sems):
    half = held[0].shape[0]
    copies = []
    for t in range(2):
        lanes = slice(t * HEAD_DIM, (t + 1) * HEAD_DIM)
        for s in range(groups):
            held[t][:, chip_column(members, groups, s)] = parts[s][:, lanes]
        copy = pltpu.make_async_copy(held[t], outs[t].at[pl.ds(h * half, half)], sems.at[t])
        copy.start()
        copies.append(copy)
    return copies


def join_first_kernel(members, groups, *refs):
    dqs, pairs = refs[:groups], refs[groups : 2 * groups]
    out, *outs = refs[2 * groups : 2 * groups + 3]
    *held, sems = refs[2 * groups + 3 :]
    copies = write_half(members, groups, 0, pairs, outs, held, sems)
    for s in range(groups):
        column = chip_column(members, groups, s)
        for n in range(out.shape[0] // BLK):
            packed = slice(n // 2 * BLK, (n // 2 + 1) * BLK)
            lanes = slice(n % 2 * HEAD_DIM, (n % 2 + 1) * HEAD_DIM)
            out[n * BLK : (n + 1) * BLK, column] = dqs[s][packed, lanes]
    for copy in copies:
        copy.wait()


def join_second_kernel(members, groups, *refs):
    outs = refs[groups + 2 : groups + 4]
    *held, sems = refs[groups + 4 :]
    for copy in write_half(members, groups, 1, refs[:groups], outs, held, sems):
        copy.wait()


def join_heads(dqs, pairs, members, groups):
    half = pairs[0].shape[0]
    vmem = pl.BlockSpec(memory_space=pltpu.VMEM)
    hbm = pl.BlockSpec(memory_space=pl.ANY)
    out = jax.ShapeDtypeStruct((2 * half, groups * HEAD_DIM), jnp.bfloat16)
    scratch = [pltpu.VMEM((half, groups * HEAD_DIM), jnp.bfloat16)] * 2
    scratch += [pltpu.SemaphoreType.DMA((2,))]
    bytes_out = 2 * half * groups * HEAD_DIM
    query_grad, key_grad, value_grad = pl.pallas_call(
        functools.partial(join_first_kernel, members, groups),
        out_shape=[out] * 3,
        in_specs=[vmem] * (2 * groups),
        out_specs=[vmem, hbm, hbm],
        scratch_shapes=scratch,
        compiler_params=pltpu.CompilerParams(vmem_limit_bytes=SMALL_LIMIT),
        cost_estimate=pl.CostEstimate(flops=0, bytes_accessed=8 * bytes_out, transcendentals=0),
        name="join_first",
    )(*dqs, *pairs[:groups])
    key_grad, value_grad = pl.pallas_call(
        functools.partial(join_second_kernel, members, groups),
        out_shape=[out] * 2,
        in_specs=[vmem] * groups + [hbm] * 2,
        out_specs=[hbm] * 2,
        scratch_shapes=scratch,
        input_output_aliases={groups: 0, groups + 1: 1},
        compiler_params=pltpu.CompilerParams(vmem_limit_bytes=SMALL_LIMIT),
        cost_estimate=pl.CostEstimate(flops=0, bytes_accessed=4 * bytes_out, transcendentals=0),
        name="join_second",
    )(*pairs[groups:], key_grad, value_grad)
    return query_grad, key_grad, value_grad


def add_kernel(members, groups, *refs):
    far = refs[: members - 1]
    own = refs[members - 1 : members - 1 + groups]
    outs = refs[members - 1 + groups :]
    half = outs[0].shape[0]
    for h in range(2):
        at = slice(h * half, (h + 1) * half)
        for s in range(groups):
            total = own[s][at, :].astype(jnp.float32)
            for part in far:
                total = total + part[s, at, :].astype(jnp.float32)
            out = outs[h * groups + s]
            out[:, :HEAD_DIM] = (total[:, :HEAD_DIM] * HEAD_DIM**-0.5).astype(jnp.bfloat16)
            out[:, HEAD_DIM:] = total[:, HEAD_DIM:].astype(jnp.bfloat16)


def add_partials(far, own, members, groups):
    vmem = pl.BlockSpec(memory_space=pltpu.VMEM)
    rows = own[0].shape[0]
    out = jax.ShapeDtypeStruct((rows // 2, 2 * HEAD_DIM), jnp.bfloat16)
    found = pl.pallas_call(
        functools.partial(add_kernel, members, groups),
        out_shape=[out] * (2 * groups),
        in_specs=[vmem] * (members - 1 + groups),
        out_specs=[vmem] * (2 * groups),
        compiler_params=pltpu.CompilerParams(vmem_limit_bytes=SMALL_LIMIT),
        cost_estimate=pl.CostEstimate(
            flops=0, bytes_accessed=8 * groups * own[0].size, transcendentals=0
        ),
        name="add_partials",
    )(*far, *own)
    return found[:groups], found[groups:]


def dot(left, right, dims):
    return lax.dot_general(left, right, (dims, ((), ())), preferred_element_type=jnp.float32)


def attend_kernel(late, near, shards, members, groups, half, *refs):
    slots = members * groups
    rows = 2 * half
    stretch = half // BLK
    links = refs[0]
    packs = [*refs[1 : 1 + groups]]
    lent = (members - 1) * (groups - 1 if late else groups // 2)
    for part in refs[1 + groups : 1 + groups + lent]:
        packs += [part.at[n] for n in range(part.shape[0])]
    refs = refs[1 + groups + lent :]
    if late:
        dq_early = refs[:groups]
        refs = refs[groups + 2 :]
        dq_outs = refs[:groups]
        own_outs = refs[groups : 2 * groups]
        far_outs = refs[2 * groups : 2 * groups + members - 1]
        refs = refs[2 * groups + members - 1 :]
    else:
        dq_outs = refs[:groups]
        refs = refs[groups:]
    pair_buf, acc, ask_buf, dq_buf, sems = refs
    device = lax.axis_index("ctx")

    moves = []
    for s in range(groups):
        moves.append((packs[s].at[pl.ds(half, half)], ask_buf.at[pl.ds(s * half, half)]))
        for r in range(members):
            i = r * groups + s
            place = pl.ds(i * rows + (half if late else 0), half)
            moves.append((packs[i].at[pl.ds(0, half)], pair_buf.at[place]))
    by_copy = 0 if near else len(moves)
    copies = all_started(moves[:by_copy], sems)
    for source, target in moves[by_copy:]:
        target[...] = source[...]
    if not late:
        acc[...] = jnp.zeros_like(acc)
    for copy in copies:
        copy.wait()

    scaling = HEAD_DIM**-0.5
    causal = lax.broadcasted_iota(jnp.int32, (BLK, BLK), 0) <= lax.broadcasted_iota(
        jnp.int32, (BLK, BLK), 1
    )

    def place_of(block):
        run = lax.div(block, stretch)
        local = block - run * stretch
        owner = run
        if late:
            is_late = run >= shards
            owner = jnp.where(is_late, 2 * shards - 1 - run, run)
            local = local + jnp.where(is_late, stretch, 0)
        bits = owner ^ device
        slot = lax.rem(bits, members) * groups + apart(lax.div(bits, members), groups)
        return pl.multiple_of(slot * rows + local * BLK, BLK)

    def step(s, _):
        asker = device ^ (apart(s, groups) * members)
        first = (2 * shards - 1 - asker if late else asker) * stretch
        units = range(stretch)
        listed = []
        for n in units:
            block = first + n
            listed.append([block, block - 1] + [links[block, i] for i in range(LINKS)])
        places = [[place_of(jnp.maximum(j, 0)) for j in row] for row in listed]
        pairs = [jnp.concatenate([pair_buf[pl.ds(p, BLK), :] for p in row], 0) for row in places]
        asks = [
            ask_buf[pl.ds(pl.multiple_of(s * half + n * BLK, BLK), BLK), :] for n in units
        ]
        raws = [dot(pairs[n][:, :HEAD_DIM], asks[n][:, :HEAD_DIM], ((1,), (1,))) for n in units]
        dprobs = [dot(pairs[n][:, HEAD_DIM:], asks[n][:, HEAD_DIM:], ((1,), (1,))) for n in units]
        dscore_b, terms = [], []
        for n in units:
            raw = [raws[n][i * BLK : (i + 1) * BLK] for i in range(SPAN)]
            dprob = dprobs[n].reshape(SPAN, BLK, BLK)
            raw[0] = jnp.where(causal, raw[0], NEG_FILL)
            unused = [0.0] + [jnp.where(j >= 0, 0.0, NEG_FILL) for j in listed[n][1:]]
            tops = [jnp.max(raw[i], axis=0, keepdims=True) + unused[i] for i in range(SPAN)]
            top = functools.reduce(jnp.maximum, tops)
            weight = jnp.stack(
                [
                    jnp.exp((raw[i] - (top - unused[i])) * scaling)
                    for i in range(SPAN)
                ]
            )
            share = 1.0 / jnp.sum(weight, axis=(0, 1), keepdims=True)
            delta = jnp.sum(weight * dprob, axis=(0, 1), keepdims=True) * share
            prob = weight * share
            dscore = (prob * (dprob - delta)).astype(jnp.bfloat16).reshape(SPAN * BLK, BLK)
            dscore_b.append(dscore)
            prob = prob.astype(jnp.bfloat16).reshape(SPAN * BLK, BLK)
            dk = dot(dscore, asks[n][:, :HEAD_DIM], ((1,), (0,)))
            dv = dot(prob, asks[n][:, HEAD_DIM:], ((1,), (0,)))
            terms.append(jnp.concatenate([dk, dv], 1))
        dq = [dot(dscore_b[n], pairs[n][:, :HEAD_DIM], ((0,), (0,))) * scaling for n in units]
        for n in units:
            lanes = slice(n % 2 * HEAD_DIM, (n % 2 + 1) * HEAD_DIM)
            packed = pl.ds(pl.multiple_of(s * (half // 2) + n // 2 * BLK, BLK), BLK)
            dq_buf[packed, lanes] = dq[n].astype(jnp.bfloat16)
            for i, p in enumerate(places[n]):
                acc[pl.ds(p, BLK), :] += terms[n][i * BLK : (i + 1) * BLK]
        return 0

    lax.fori_loop(0, groups, step, 0, unroll=4)

    quarter = half // 2
    for s in range(groups):
        if late:
            dq_outs[s][:quarter] = dq_early[s][...]
        start = quarter if late else 0
        dq_outs[s][start : start + quarter] = dq_buf[s * quarter : (s + 1) * quarter, :]
    if late:
        for s in range(groups):
            own_outs[s][...] = acc[s * rows : (s + 1) * rows, :].astype(jnp.bfloat16)
        for r in range(1, members):
            for s in range(groups):
                start = (r * groups + s) * rows
                far_outs[r - 1][s] = acc[start : start + rows, :].astype(jnp.bfloat16)


def attend(links, packs, dq_early, buffers, rows, shards, members, groups):
    late = len(buffers) > 0
    half = rows // 2
    slots = members * groups
    blocks = groups * half // BLK
    near = slots * rows <= 4096

    def shape(*dims, dtype=jnp.bfloat16):
        return jax.ShapeDtypeStruct((*dims, 2 * HEAD_DIM), dtype)

    outs = [shape(half if late else half // 2)] * groups
    if late:
        outs += [shape(rows)] * groups + [shape(groups, rows)] * (members - 1)
    outs += [shape(slots * rows), shape(slots * rows, dtype=jnp.float32)]
    vmem = pl.BlockSpec(memory_space=pltpu.VMEM)
    read = vmem if near else pl.BlockSpec(memory_space=pl.ANY)
    given = [*packs, *dq_early, *buffers]
    found = pl.pallas_call(
        functools.partial(attend_kernel, late, near, shards, members, groups, half),
        out_shape=outs,
        in_specs=[pl.BlockSpec(memory_space=pltpu.SMEM)]
        + [read] * len(packs)
        + [vmem] * (len(dq_early) + len(buffers)),
        out_specs=[vmem] * len(outs),
        input_output_aliases={len(given) - 1: len(outs) - 2, len(given): len(outs) - 1}
        if late
        else {},
        scratch_shapes=[
            pltpu.VMEM((groups * half, 2 * HEAD_DIM), jnp.bfloat16),
            pltpu.VMEM((groups * half // 2, 2 * HEAD_DIM), jnp.bfloat16),
            pltpu.SemaphoreType.DMA((slots + groups,)),
        ],
        compiler_params=pltpu.CompilerParams(vmem_limit_bytes=SMALL_LIMIT),
        cost_estimate=pl.CostEstimate(
            flops=10 * blocks * SPAN * BLK * BLK * HEAD_DIM if late else 0,
            bytes_accessed=8 * slots * rows * HEAD_DIM if late else 0,
            transcendentals=blocks * SPAN * BLK * BLK if late else 0,
        ),
        name="attend_late" if late else "attend_early",
    )(links, *given)
    if late:
        return found[:groups], found[groups : 2 * groups], found[2 * groups : -2]
    return found[:groups], found[-2:]


def to_chips(parts, members):
    groups = len(parts)
    return [swapped(part, -s % groups * members) if s else part for s, part in enumerate(parts)]


def with_members(parts, members):
    return [swapped(part, r) for r in range(1, members) for part in parts]


def per_device(query, key, value, out_grad, links):
    rows, width = query.shape
    groups = width // HEAD_DIM
    shards = lax.axis_size("ctx")
    members = shards // groups
    arrays = (query, key, value, out_grad)

    early, late = split_heads(arrays, members, groups)
    early = to_chips(early, members)
    late = to_chips(late, members)
    early = early + with_members(only_pairs(early, rows // 2, [], 2), members)
    dq_early, buffers = attend(links, early, [], [], rows, shards, members, groups)
    lent = only_pairs(late[:2], rows // 2, dq_early[:1], 2)
    for s in range(2, groups):
        lent += only_pairs(late[s : s + 1], rows // 2, dq_early[:1], 1)
    late = late + with_members(lent, members)
    dqs, own, far = attend(links, late, dq_early, buffers, rows, shards, members, groups)
    far = [swapped(part, r) for r, part in enumerate(far, 1)]
    dqs = to_chips(dqs, members)
    pairs = add_partials(far, own, members, groups)
    pairs = to_chips(pairs[0], members) + to_chips(pairs[1], members)
    return join_heads(dqs, pairs, members, groups)


def solution(mesh):
    return jax.shard_map(
        per_device,
        mesh=mesh,
        in_specs=(P("ctx", "head"), P("ctx", "head"), P("ctx", "head"), P("ctx", "head"), P()),
        out_specs=(P("ctx", "head"), P("ctx", "head"), P("ctx", "head")),
        check_vma=False,
    )
```
